256 devices in a mesh: expert: 128 (over x, z, y), tensor: 2 (over core).
Axes of the slice: x: 4, y: 4, z: 8, core: 2. Of those that a mesh axis runs over, the one named last changes fastest.
Arguments:
- context: bfloat16 [32768, 1664], P('expert', 'tensor'), may hold values from -6 to 6
- out_weight: bfloat16 [1664, 1664], P('tensor'), may hold values from -0.15625 to 0.15625
- residual: bfloat16 [32768, 1664], P(('expert', 'tensor')), may hold values from -6 to 6
- norm_gain: float32 [1664], replicated, may hold values from 0.1 to 1.9
- expert_in: bfloat16 [128, 1664, 2048], P('expert', None, 'tensor'), may hold values from -0.15625 to 0.15625
- expert_out: bfloat16 [128, 2048, 1664], P('expert', 'tensor'), may hold values from -0.0625 to 0.0625
- patch_index: int32 [32, 512], replicated, may hold values from 0 to 32767, as said below
- patch_count: int32 [32], replicated, may hold values from 256 to 512, as said below
- gate_value: float32 [32, 512], replicated, may hold values from 0.2 to 1
- upstream: bfloat16 [32768, 1664], P(('expert', 'tensor')), may hold values from -6 to 6
Outputs:
- layer_out: bfloat16 [32768, 1664], P(('expert', 'tensor'))
- stream_grad: bfloat16 [32768, 1664], P(('expert', 'tensor'))
The draws below stay inside these ranges and needn't reach their ends.
Inputs may be any that keep to these rules, and one draw needn't show every extreme that they name: `patch_index`: the first patch_count[e] slots of expert e's list hold distinct patch numbers below 32768, the other slots 0. Among the patches of one aligned block of 256 patches, at most 4 are listed by one expert, and some expert lists exactly 4 from every block. `patch_count`: some expert's list is full.
All inputs are finite; a program needn't handle non-finite values.
Results may differ from the reference program's by a relative error of at most 0.0045.
Values may be sent and summed in bfloat16 or wider, within the bound.
No kernel may reach another device: no remote copies, remote signals or barrier semaphores. Data moves between devices by JAX's collectives and lax.ppermute only.
A program may use at most 64 MiB of HBM per device.

```python
import jax
import jax.numpy as jnp
from jax import lax

D = 1664
FF = 8192
HEADS = 16
HEAD_DIM = 104
SHARDS = 4
TOK_DEV = 256
SEND = 4
EXPERTS = 32
TOKENS = 32768
CAP = 512
N_TENSOR = 2


def routing_tables(key):
    sources = TOKENS // TOK_DEV
    key_count, key_full, key_rows, key_order = jax.random.split(key, 4)
    per_block = jax.random.randint(key_count, (EXPERTS, sources), SEND // 2, SEND + 1)
    full_expert = jax.random.randint(key_full, (), 0, EXPERTS)
    light_expert = (full_expert + 1) % EXPERTS
    expert_ids = jnp.arange(EXPERTS)[:, None]
    per_block = jnp.where(expert_ids == full_expert, SEND, per_block)
    per_block = jnp.where(expert_ids == light_expert, SEND // 2, per_block)
    row_keys = jax.random.split(key_rows, EXPERTS * sources)
    picked = jax.vmap(lambda sub_key: jax.random.permutation(sub_key, TOK_DEV)[:SEND])(row_keys)
    picked = picked.reshape(EXPERTS, sources, SEND)
    rotated = (picked - picked[:, :, :1] + TOK_DEV - 1) % TOK_DEV
    picked = jnp.where((expert_ids == full_expert)[:, :, None], rotated, picked)
    patches = picked + (jnp.arange(sources) * TOK_DEV)[None, :, None]
    used_slot = jnp.arange(SEND)[None, None, :] < per_block[:, :, None]
    flat_patch = patches.reshape(EXPERTS, sources * SEND)
    flat_used = used_slot.reshape(EXPERTS, sources * SEND)
    order_keys = jax.random.split(key_order, EXPERTS)
    scores = jax.vmap(lambda sub_key: jax.random.permutation(sub_key, sources * SEND))(order_keys)
    scores = jnp.where(flat_used, scores, sources * SEND + jnp.arange(sources * SEND)[None, :])
    order_ids = jnp.argsort(scores, axis=1, stable=True)
    listed = jnp.take_along_axis(flat_patch, order_ids, axis=1)
    counts = jnp.sum(per_block, axis=1)
    slot_ids = jnp.arange(sources * SEND)
    listed = jnp.where(slot_ids[None, :] < counts[:, None], listed, 0)
    return (listed.astype(jnp.int32), counts.astype(jnp.int32))


def draw_patch_index(key, part):
    tables = routing_tables(key)
    return tables[0]


def draw_patch_count(key, part):
    tables = routing_tables(key)
    return tables[1]


def steps_of(own_key, dims, shards, least, top_value):
    factor_of = 1.0
    for axis_at, shards_of in shards:
        draws = jax.random.uniform(jax.random.fold_in(jax.random.fold_in(own_key, 6), axis_at), (shards_of,), jnp.float32, least / len(shards), top_value / len(shards))
        factor_of = factor_of * jnp.repeat(jnp.exp(draws), dims[axis_at] // shards_of).reshape((-1,) + (1,) * (len(dims) - 1 - axis_at))
    return factor_of


def bell_draw(stream_key, shape, scale, reach, pieces=(), kind=jnp.bfloat16):
    drawn = jax.random.normal(stream_key, shape, jnp.float32) * scale
    if len(pieces) > 0:
        drawn = steps_of(stream_key, shape, pieces, -0.22, 0.18) * drawn
    return jnp.clip(drawn, min=-reach, max=reach).astype(kind)


def setup_inputs(seed: int = 0) -> dict:
    seeds = jax.random.split(jax.random.key(seed), 11)
    context = bell_draw(seeds[0], (TOKENS, HEADS * HEAD_DIM), 1.0, 6.0, ((0, 128), (1, 2)))
    out_weight = bell_draw(seeds[1], (HEADS * HEAD_DIM, D), (HEADS * HEAD_DIM) ** -0.5, 0.15625, ((0, 2),))
    residual = bell_draw(seeds[2], (TOKENS, D), 1.0, 6.0, ((0, 256),))
    norm_gain = jnp.clip(1.0 + 0.18 * jax.random.normal(seeds[3], (D,), jnp.float32), 0.1, 1.9)
    expert_in = bell_draw(seeds[4], (EXPERTS * SHARDS, D, FF // SHARDS), D ** -0.5, 0.15625, ((0, 128), (2, 2)))
    expert_out = bell_draw(seeds[5], (EXPERTS * SHARDS, FF // SHARDS, D), FF ** -0.5, 0.0625, ((0, 128), (1, 2)))
    patch_index = draw_patch_index(jax.random.fold_in(seeds[10], 71), 0)
    patch_count = draw_patch_count(jax.random.fold_in(seeds[10], 71), 0)
    gate_value = jnp.clip(jax.random.uniform(seeds[8], (EXPERTS, CAP), jnp.float32, 0.2, 1.0), 0.2, 1.0)
    upstream = bell_draw(seeds[9], (TOKENS, D), 1.0, 6.0, ((0, 256),))
    return {"context": context, "out_weight": out_weight, "residual": residual, "norm_gain": norm_gain, "expert_in": expert_in, "expert_out": expert_out, "patch_index": patch_index, "patch_count": patch_count, "gate_value": gate_value, "upstream": upstream}


def norm_rows(stream, norm_gain):
    center_mean = lax.optimization_barrier(jnp.mean(stream, axis=-1, keepdims=True))
    centered = stream - center_mean
    variance = lax.optimization_barrier(jnp.mean(centered * centered, axis=-1, keepdims=True))
    return norm_gain * centered * lax.rsqrt(variance + 1e-06)

def gelu_act(values):
    return jax.nn.gelu(values, approximate=True)

def reference(context, out_weight, residual, norm_gain, expert_in, expert_out, patch_index, patch_count, gate_value, upstream):
    attended = jnp.dot(context, out_weight, preferred_element_type=jnp.float32)
    stream = residual.astype(jnp.float32) + attended
    normed = lax.optimization_barrier(norm_rows(stream, norm_gain).astype(jnp.bfloat16))
    groups = SHARDS * N_TENSOR
    unit_block = FF // groups
    weight_in = expert_in.reshape(EXPERTS, SHARDS, D, FF // SHARDS).transpose(0, 2, 1, 3).reshape(EXPERTS, D, FF)
    weight_out = expert_out.reshape(EXPERTS, FF, D)
    slot_live = jnp.arange(CAP)[None, :] < patch_count[:, None]
    slot_gate = jnp.where(slot_live, gate_value, jnp.zeros_like(gate_value))

    def one_expert(carry, expert_item):
        mixed_rows, back_rows = carry
        index_row, gate_row, first_weight, second_weight = expert_item
        first_full = first_weight.astype(jnp.float32)
        second_full = second_weight.astype(jnp.float32)
        taken = normed[index_row].astype(jnp.float32)
        pre_act = jnp.dot(taken, first_full)
        hidden = lax.optimization_barrier(gelu_act(pre_act).astype(jnp.bfloat16)).astype(jnp.float32)
        parts = jnp.einsum('cgf,gfd->gcd', hidden.reshape(CAP, groups, unit_block), second_full.reshape(groups, unit_block, D))
        parts = lax.optimization_barrier(parts.astype(jnp.bfloat16)).astype(jnp.float32)
        result = lax.optimization_barrier(jnp.sum(parts, axis=0))
        down_rows = upstream[index_row].astype(jnp.float32)
        hidden_grad = jnp.dot(down_rows, second_full.T)
        pre_grad = jax.vjp(gelu_act, pre_act)[1](hidden_grad)[0]
        pre_grad = lax.optimization_barrier(pre_grad.astype(jnp.bfloat16)).astype(jnp.float32)
        back_parts = jnp.einsum('cgf,dgf->gcd', pre_grad.reshape(CAP, groups, unit_block), first_full.reshape(D, groups, unit_block))
        back_parts = lax.optimization_barrier(back_parts.astype(jnp.bfloat16)).astype(jnp.float32)
        back_sum = lax.optimization_barrier(jnp.sum(back_parts, axis=0))
        mixed_rows = mixed_rows.at[index_row].add(gate_row[:, None] * result)
        back_rows = back_rows.at[index_row].add(gate_row[:, None] * back_sum)
        return ((mixed_rows, back_rows), None)
    zeros_rows = jnp.zeros((TOKENS, D), jnp.float32)
    totals, unused = lax.scan(one_expert, (zeros_rows, zeros_rows), (patch_index, slot_gate, weight_in, weight_out))
    mixed_rows, back_rows = totals
    layer_out = (stream + mixed_rows).astype(jnp.bfloat16)
    pull_back = jax.vjp(lambda values: norm_rows(values, norm_gain), stream)[1]
    stream_grad = (upstream.astype(jnp.float32) + pull_back(back_rows)[0]).astype(jnp.bfloat16)
    return (layer_out, stream_grad)
```

```python
import jax
import jax.numpy as jnp
from jax import lax
from jax.sharding import Mesh, PartitionSpec as P

SLOTS = 4
HALF = 2
BF = jnp.bfloat16
F32 = jnp.float32


def norm_rows(stream, norm_gain):
    center_mean = jnp.mean(stream, axis=-1, keepdims=True)
    centered = stream - center_mean
    variance = jnp.mean(centered * centered, axis=-1, keepdims=True)
    return norm_gain * centered * lax.rsqrt(variance + 1e-06)


def gelu_act(values):
    return jax.nn.gelu(values, approximate=True)


def mm(a, b):
    return jnp.dot(a, b, preferred_element_type=F32)


def mm_t(a, b):
    return lax.dot_general(a, b, (((1,), (1,)), ((), ())), preferred_element_type=F32)


def swap_core(x):
    return lax.ppermute(x, "core", [(0, 1), (1, 0)])


def shift_y(x, step):
    size = lax.axis_size("y")
    return lax.ppermute(x, "y", [(i, (i + step) % size) for i in range(size)])


def per_device(
    context,
    out_weight,
    residual,
    norm_gain,
    expert_in,
    expert_out,
    patch_index,
    patch_count,
    gate_value,
    upstream,
):
    own_rows, width = residual.shape
    experts, capacity = patch_index.shape
    core = lax.axis_index("core")
    index = lax.axis_index("xz") * lax.axis_size("y") + lax.axis_index("y")
    first_patch = index * (2 * own_rows)

    with jax.named_scope("routing"):
        local_row = patch_index - first_patch
        listed = jnp.arange(capacity)[None, :] < patch_count[:, None]
        mine = listed & (local_row >= 0) & (local_row < 2 * own_rows)
        upto = (jnp.arange(capacity)[:, None] <= jnp.arange(capacity)[None, :]).astype(BF)
        rank = mm(mine.astype(BF), upto).astype(jnp.int32) - 1
        picked = mine[:, None, :] & (rank[:, None, :] == jnp.arange(SLOTS)[None, :, None])
        row_of = jnp.sum(jnp.where(picked, local_row[:, None, :] + 1, 0), axis=2) - 1
        weight_of = jnp.sum(jnp.where(picked, gate_value[:, None, :], 0.0), axis=2)
        row_keep = jnp.where(core == 0, row_of[:, :HALF], row_of[:, HALF:]).reshape(-1)
        row_send = jnp.where(core == 0, row_of[:, HALF:], row_of[:, :HALF]).reshape(-1)
        weight_keep = jnp.where(core == 0, weight_of[:, :HALF], weight_of[:, HALF:]).reshape(-1)
        weight_send = jnp.where(core == 0, weight_of[:, HALF:], weight_of[:, :HALF]).reshape(-1)
        own_ids = core * own_rows + jnp.arange(own_rows)
        hot_keep = row_keep[:, None] == own_ids[None, :]
        hot_send = row_send[:, None] == own_ids[None, :]
        pick_keep = hot_keep.astype(BF)
        pick_send = hot_send.astype(BF)
        spread = jnp.concatenate(
            [
                jnp.where(hot_keep, weight_keep[:, None], 0.0).T,
                jnp.where(hot_send, weight_send[:, None], 0.0).T,
            ],
            axis=1,
        )
        spread_high = spread.astype(BF)
        spread_low = (spread - spread_high.astype(F32)).astype(BF)

    def dispatch(rows_own):
        theirs = swap_core(mm(pick_send, rows_own).astype(BF))
        chosen = mm(pick_keep, rows_own).astype(BF) + theirs
        chosen = chosen.reshape(experts, HALF, width)
        got = lax.all_to_all(chosen, "xz", split_axis=0, concat_axis=0, tiled=True)
        return got.reshape(experts * HALF, width)

    def gather_y(block):
        half = block.shape[0] // 2
        before = shift_y(block, 1)
        after = shift_y(block, -1)
        far_top = shift_y(before[:half], 1)
        far_bottom = shift_y(after[half:], -1)
        return jnp.concatenate([block, after, far_top, far_bottom, before], axis=0)

    def reduce_y(parts):
        block = parts.shape[0] // 4
        half = block // 2
        own, after, far, before = (parts[i * block : (i + 1) * block] for i in range(4))
        from_before = shift_y(far[:half].astype(BF), 1)
        from_after = shift_y(far[half:].astype(BF), -1)
        after = jnp.concatenate([after[:half] + from_before.astype(F32), after[half:]], axis=0)
        before = jnp.concatenate([before[:half], before[half:] + from_after.astype(F32)], axis=0)
        left = shift_y(after.astype(BF), 1)
        right = shift_y(before.astype(BF), -1)
        return own + left.astype(F32) + right.astype(F32)

    def give_back(keep_part, send_part):
        theirs = swap_core(send_part.astype(BF))
        total = reduce_y(keep_part + theirs.astype(F32)).astype(BF)
        total = total.reshape(experts, HALF, width)
        got = lax.all_to_all(total, "xz", split_axis=0, concat_axis=0, tiled=True)
        got = got.reshape(experts * HALF, width)
        rows = jnp.concatenate([got, swap_core(got)], axis=0)
        return mm(spread_high, rows) + mm(spread_low, rows)

    with jax.named_scope("dispatch_upstream"):
        down_keep = gather_y(dispatch(upstream))
        down_send = swap_core(down_keep)

    with jax.named_scope("attend"):
        context_send = lax.dynamic_slice_in_dim(context, (1 - core) * own_rows, own_rows, 0)
        context_keep = lax.dynamic_slice_in_dim(context, core * own_rows, own_rows, 0)
        theirs = swap_core(mm(context_send, out_weight))
        stream = residual.astype(F32) + (mm(context_keep, out_weight) + theirs)
        normed = norm_rows(stream, norm_gain).astype(BF)

    with jax.named_scope("dispatch_normed"):
        rows_keep = gather_y(dispatch(normed))
        rows_send = swap_core(rows_keep)

    weight_in = expert_in[0]
    weight_out = expert_out[0]
    with jax.named_scope("experts"):
        pre_keep = mm(rows_keep, weight_in)
        pre_send = mm(rows_send, weight_in)
        part_send = mm(gelu_act(pre_send).astype(BF), weight_out)
        part_keep = mm(gelu_act(pre_keep).astype(BF), weight_out)
    with jax.named_scope("return_result"):
        mixed = give_back(part_keep, part_send)
        layer_out = (stream + mixed).astype(BF)

    with jax.named_scope("experts_back"):
        hidden_grad_send = mm_t(down_send, weight_out)
        hidden_grad_keep = mm_t(down_keep, weight_out)
        pre_grad_send = jax.vjp(gelu_act, pre_send)[1](hidden_grad_send)[0].astype(BF)
        pre_grad_keep = jax.vjp(gelu_act, pre_keep)[1](hidden_grad_keep)[0].astype(BF)
        back_send = mm_t(pre_grad_send, weight_in)
        back_keep = mm_t(pre_grad_keep, weight_in)
    with jax.named_scope("return_back"):
        back_rows = give_back(back_keep, back_send)
        pull_back = jax.vjp(lambda values: norm_rows(values, norm_gain), stream)[1]
        stream_grad = (upstream.astype(F32) + pull_back(back_rows)[0]).astype(BF)
    return (layer_out, stream_grad)


def solution(mesh):
    sizes = mesh.devices.shape
    shards = 4
    split = Mesh(
        mesh.devices.reshape(sizes[0] // shards, shards, sizes[1]), ("xz", "y", "core")
    )
    return jax.shard_map(
        per_device,
        mesh=split,
        in_specs=(
            P(("xz", "y"), "core"),
            P("core", None),
            P(("xz", "y", "core"), None),
            P(),
            P(("xz", "y"), None, "core"),
            P(("xz", "y"), "core", None),
            P(),
            P(),
            P(),
            P(("xz", "y", "core"), None),
        ),
        out_specs=(P(("xz", "y", "core"), None), P(("xz", "y", "core"), None)),
        check_vma=False,
    )
```

```python
import jax
import jax.numpy as jnp
from jax import lax
from jax.experimental import pallas as pl
from jax.experimental.pallas import tpu as pltpu
from jax.sharding import Mesh, PartitionSpec as P

SLOTS = 4
HALF = 2
BF = jnp.bfloat16
F32 = jnp.float32
I32 = jnp.int32
VMEM = pl.BlockSpec(memory_space=pltpu.VMEM)
SMEM = pl.BlockSpec(memory_space=pltpu.SMEM)
WIDE = 896
PACK = 8


def mm(a, b):
    return jnp.dot(a, b, preferred_element_type=F32)


def mm_t(a, b):
    return lax.dot_general(a, b, (((1,), (1,)), ((), ())), preferred_element_type=F32)


def cuts(size, step):
    return [(i, min(i + step, size)) for i in range(0, size, step)]


def iota(shape, dim):
    return lax.broadcasted_iota(I32, shape, dim)


def call(kernel, outs, in_specs, scratch=(), flops=0, moved=0, mib=16):
    return pl.pallas_call(
        kernel,
        out_shape=outs,
        in_specs=in_specs,
        out_specs=jax.tree.map(lambda _: VMEM, outs),
        scratch_shapes=list(scratch),
        compiler_params=pltpu.CompilerParams(vmem_limit_bytes=mib * 2**20),
        cost_estimate=pl.CostEstimate(flops=flops, bytes_accessed=moved, transcendentals=0),
    )


def attend_kernel(ids, context, weight, send, keep):
    core = ids[0]
    rows = send.shape[0]
    for out, at in ((send, 1 - core), (keep, core)):
        block = context[pl.ds(pl.multiple_of(at * rows, rows), rows), :]
        for lo, hi in cuts(out.shape[1], 512):
            out[:, lo:hi] = mm(block, weight[:, lo:hi])


def routing_kernel(ids, index, count, gate, pick_keep, pick_send, merge_high, merge_low):
    core = ids[0]
    experts, capacity = index.shape
    packed = experts * PACK
    own_rows = 128
    local = index[...] - ids[1]
    listed = iota((experts, capacity), 1) < count[...]
    mine = listed & (local >= 0) & (local < 2 * own_rows)
    upto = jnp.where(iota((capacity, capacity), 0) <= iota((capacity, capacity), 1), 1.0, 0.0)
    rank = mm(jnp.where(mine, 1.0, 0.0).astype(BF), upto.astype(BF))
    lane = iota((experts, 128), 1)
    rows = jnp.zeros((experts, 128), F32)
    gates = jnp.zeros((experts, 128), F32)
    shifted = (local + 1).astype(F32)
    for slot in range(SLOTS):
        here = mine & (rank == slot + 1.0)
        row = jnp.sum(jnp.where(here, shifted, 0.0), axis=1, keepdims=True) - 1.0
        rows = jnp.where(lane == slot, row, rows)
        weight = jnp.sum(jnp.where(here, gate[...], 0.0), axis=1, keepdims=True)
        gates = jnp.where(lane == slot, weight, gates)
    rows = rows.astype(BF)
    gate_high = gates.astype(BF)
    gate_low = (gates - gate_high.astype(F32)).astype(BF)
    spread = jnp.where(iota((packed, experts), 0) // PACK == iota((packed, experts), 1), 1.0, 0.0).astype(BF)
    down = mm(spread, rows)
    r_col = iota((packed, 128), 0) % PACK
    lane_id = iota((packed, 128), 1)
    k = iota((packed, 2 * own_rows), 1)
    r_wide = iota((packed, 2 * own_rows), 0) % PACK
    same_stream = (r_wide // 2) % 2 == k // own_rows
    patch = (core * own_rows + k % own_rows).astype(F32)
    for out, side in ((pick_keep, core), (pick_send, 1 - core)):
        slot = 2 * side + r_col % 2
        row = jnp.sum(jnp.where(lane_id == slot, down, 0.0), axis=1, keepdims=True)
        hot = same_stream & (row == patch)
        out[:, : 2 * own_rows] = jnp.where(hot & (r_wide < 4), 1.0, 0.0).astype(BF)
        out[:, 2 * own_rows :] = jnp.where(hot & (r_wide >= 4), 1.0, 0.0).astype(BF)
    along = (((0,), (1,)), ((), ()))
    across = [
        lax.dot_general(part, spread, along, preferred_element_type=F32)
        for part in (rows, gate_high, gate_low)
    ]
    q = iota((128, packed), 1) % PACK
    sub = iota((128, packed), 0)
    own = (core * own_rows + iota((own_rows, packed), 0)).astype(F32)
    for which, side in ((0, core), (1, 1 - core)):
        slot = 2 * side + q % 2
        row, high, low = (
            jnp.sum(jnp.where(sub == slot, part, 0.0), axis=0, keepdims=True) for part in across
        )
        hot = row == own
        for group in range(4):
            here = hot & (q // 2 == group)
            at = (slice(group * own_rows, (group + 1) * own_rows), slice(which * packed, (which + 1) * packed))
            merge_high[at] = jnp.where(here, high, 0.0).astype(BF)
            merge_low[at] = jnp.where(here, low, 0.0).astype(BF)


def statistics(stream):
    mean = jnp.mean(stream, axis=-1, keepdims=True)
    centered = stream - mean
    variance = jnp.mean(centered * centered, axis=-1, keepdims=True)
    return centered, lax.rsqrt(variance + 1e-06)


def norm_kernel(att_keep, att_got, residual, gain, upstream, pick_keep, pick_send, stream, keep, send, both):
    rows, width = residual.shape
    total = residual[...].astype(F32) + (att_keep[...] + att_got[...])
    stream[...] = total
    centered, inverse = statistics(total)
    both[:rows, :] = (gain[...] * centered * inverse).astype(BF)
    both[rows:, :] = upstream[...]
    rest = width - WIDE
    for pick, out in ((pick_send, send), (pick_keep, keep)):
        first, second = pick[:, : 2 * rows], pick[:, 2 * rows :]
        out[:, :rest] = (mm(first, both[:, :rest]) + mm(second, both[:, WIDE:])).astype(BF)
        out[:, rest:] = mm(first, both[:, rest:WIDE]).astype(BF)


def place(packed):
    q = packed
    return (q % 64 // 2) * PACK + q // 64 * 2 + q % 2


def unpack_kernel(got, first, second):
    n = got.shape[0]
    order = jnp.where(place(iota((n, n), 0)) == iota((n, n), 1), 1.0, 0.0).astype(BF)
    flat = mm(order, got[...]).astype(BF)
    quarter = n // 4
    rest = first.shape[1] - WIDE
    for stream, out in enumerate((first, second)):
        out[:, :WIDE] = flat[stream * quarter : (stream + 1) * quarter, :]
        out[:, WIDE:] = flat[(2 + stream) * quarter : (3 + stream) * quarter, :rest]


def pack_kernel(own_r, one_r, two_r, own_b, one_b, two_b, out, flat):
    n = out.shape[0]
    quarter = n // 4
    rest = own_r.shape[1] - WIDE
    flat[2 * quarter :, rest:] = jnp.zeros((2 * quarter, WIDE - rest), BF)
    for stream, (own, one, two) in enumerate(((own_r, one_r, two_r), (own_b, one_b, two_b))):
        total = (own[...] + one[...].astype(F32) + two[...].astype(F32)).astype(BF)
        flat[stream * quarter : (stream + 1) * quarter, :] = total[:, :WIDE]
        flat[(2 + stream) * quarter : (3 + stream) * quarter, :rest] = total[:, WIDE:]
    order = jnp.where(iota((n, n), 0) == place(iota((n, n), 1)), 1.0, 0.0).astype(BF)
    out[...] = mm(order, flat[...]).astype(BF)


def forward_kernel(x0, x1, x2, x3, w1, w2, slope, part, x, hidden):
    block = x0.shape[0]
    for i, ref in enumerate((x0, x1, x2, x3)):
        x[i * block : (i + 1) * block, :] = ref[...]
    for lo, hi in cuts(hidden.shape[1], 256):
        v = mm(x[...], w1[:, lo:hi])
        square = v * v
        t = jnp.tanh(0.7978845608 * v * (1.0 + 0.044715 * square))
        gate = 0.5 + 0.5 * t
        hidden[:, lo:hi] = (v * gate).astype(BF)
        slope[:, lo:hi] = gate + 0.5 * v * (1.0 - t * t) * (0.7978845608 * (1.0 + 0.134145 * square))
    for lo, hi in cuts(part.shape[1], 512):
        part[:, lo:hi] = mm(hidden[...], w2[:, lo:hi]).astype(part.dtype)


def backward_kernel(x0, x1, x2, x3, w1, w2, slope, part, x, grad):
    block = x0.shape[0]
    for i, ref in enumerate((x0, x1, x2, x3)):
        x[i * block : (i + 1) * block, :] = ref[...]
    for lo, hi in cuts(grad.shape[1], 256):
        grad[:, lo:hi] = (mm_t(x[...], w2[lo:hi, :]) * slope[:, lo:hi]).astype(BF)
    for lo, hi in cuts(part.shape[1], 512):
        part[:, lo:hi] = mm_t(grad[...], w1[lo:hi, :]).astype(part.dtype)


def combine_kernel(keep, got, own, one, two, far):
    block = own.shape[0]
    for i, out in enumerate((own, one, two, far)):
        at = slice(i * block, (i + 1) * block)
        out[...] = (keep[at, :] + got[at, :].astype(F32)).astype(out.dtype)


def add_kernel(a, b, out):
    out[...] = (a[...].astype(F32) + b[...].astype(F32)).astype(BF)


def final_kernel(mine, theirs, merge_high, merge_low, stream, gain, upstream, layer_out, stream_grad, back):
    rows, width = stream.shape
    n = mine.shape[0]
    rest = width - WIDE
    total = stream[...]
    centered, inverse = statistics(total)
    x_hat = centered * inverse
    for group in range(4):
        at = slice(group * rows, (group + 1) * rows)
        summed = mm(merge_high[at, :n], mine[...]) + mm(merge_high[at, n:], theirs[...])
        summed += mm(merge_low[at, :n], mine[...]) + mm(merge_low[at, n:], theirs[...])
        cols = slice(0, WIDE) if group < 2 else slice(WIDE, width)
        summed = summed if group < 2 else summed[:, :rest]
        if group % 2 == 0:
            layer_out[:, cols] = (total[:, cols] + summed).astype(BF)
        else:
            back[:, cols] = summed
    scaled = gain[...] * back[...]
    mean = jnp.mean(scaled, axis=-1, keepdims=True)
    along = jnp.mean(scaled * x_hat, axis=-1, keepdims=True)
    pulled = inverse * (scaled - mean - x_hat * along)
    stream_grad[...] = (upstream[...].astype(F32) + pulled).astype(BF)


def per_device(
    context,
    out_weight,
    residual,
    norm_gain,
    expert_in,
    expert_out,
    patch_index,
    patch_count,
    gate_value,
    upstream,
):
    rows, width = residual.shape
    experts, capacity = patch_index.shape
    shards = lax.axis_size("y")
    packed = experts * PACK
    block = experts * HALF
    units = expert_in.shape[2]
    sds = jax.ShapeDtypeStruct
    core = lax.axis_index("core")
    index = lax.axis_index("xz") * shards + lax.axis_index("y")
    ids = jnp.stack([core, index * (2 * rows)]).astype(I32)
    gain = norm_gain.reshape(1, width)

    def swap_core(x):
        return lax.ppermute(x, "core", [(0, 1), (1, 0)])

    def ring(x, way):
        pairs = []
        for y in range(shards):
            for c in range(2):
                step = way if c == 0 else -way
                pairs.append((y * 2 + c, (y + step) % shards * 2 + c))
        return lax.ppermute(x, ("y", "core"), pairs)

    def exchange(x):
        got = lax.all_to_all(
            x.reshape(experts, PACK, WIDE), "xz", split_axis=0, concat_axis=0, tiled=True
        )
        return got.reshape(packed, WIDE)

    with jax.named_scope("attend"):
        att_send, att_keep = call(
            attend_kernel,
            [sds((rows, width), F32)] * 2,
            [SMEM, VMEM, VMEM],
            flops=4 * rows * width * context.shape[1],
            moved=5 * 10**6,
        )(ids, context, out_weight)
        att_got = swap_core(att_send)
    with jax.named_scope("routing"):
        pick_keep, pick_send, merge_high, merge_low = call(
            routing_kernel,
            [sds((packed, 4 * rows), BF)] * 2 + [sds((4 * rows, 2 * packed), BF)] * 2,
            [SMEM] + [VMEM] * 3,
            flops=10**9,
            moved=2 * 10**6,
        )(ids, patch_index, patch_count.reshape(experts, 1), gate_value)
    with jax.named_scope("norm"):
        stream, keep, send = call(
            norm_kernel,
            [sds((rows, width), F32)] + [sds((packed, WIDE), BF)] * 2,
            [VMEM] * 7,
            [pltpu.VMEM((2 * rows, width), BF)],
            flops=10**9,
            moved=3 * 10**6,
        )(att_keep, att_got, residual, gain, upstream, pick_keep, pick_send)
    with jax.named_scope("dispatch"):
        got = exchange(keep + swap_core(send))
        normed_rows, down_rows = call(
            unpack_kernel, [sds((block, width), BF)] * 2, [VMEM], flops=10**8, moved=10**6
        )(got)

    def gather_y(own):
        one = ring(own, 1)
        two = ring(own, -1)
        far = ring(one, 1)
        keeps = [own, one, two, far]
        return keeps, [swap_core(x) for x in keeps]

    def combine(keep_part, send_part):
        return call(
            combine_kernel,
            [sds((block, width), F32)] * 2 + [sds((block, width), BF)] * 2,
            [VMEM] * 2,
            flops=10**6,
            moved=4 * 10**6,
        )(keep_part, swap_core(send_part))

    def reduce_y(parts):
        own, one, two, far = parts
        from_two = ring(two, 1)
        from_far = ring(far, -1)
        one = call(add_kernel, sds((block, width), BF), [VMEM] * 2, flops=10**5, moved=10**6)(one, from_far)
        return own, ring(one, -1), from_two

    weight_in = expert_in[0]
    weight_out = expert_out[0]
    tall = shards * block
    flops = 4 * tall * width * units

    def forward(xs, kind):
        return call(
            forward_kernel,
            [sds((tall, units), F32), sds((tall, width), kind)],
            [VMEM] * 6,
            [pltpu.VMEM((tall, width), BF), pltpu.VMEM((tall, units), BF)],
            flops=flops,
            moved=10**7,
            mib=24,
        )(*xs, weight_in, weight_out)

    def backward(xs, slope, kind):
        return call(
            backward_kernel,
            sds((tall, width), kind),
            [VMEM] * 7,
            [pltpu.VMEM((tall, width), BF), pltpu.VMEM((tall, units), BF)],
            flops=flops,
            moved=10**7,
            mib=24,
        )(*xs, weight_in, weight_out, slope)

    with jax.named_scope("gather_normed"):
        keeps, sends = gather_y(normed_rows)
    with jax.named_scope("gather_down"):
        down_keeps, down_sends = gather_y(down_rows)
    with jax.named_scope("forward"):
        slope_send, part_send = forward(sends, BF)
        slope_keep, part_keep = forward(keeps, F32)
    with jax.named_scope("return_result"):
        result = reduce_y(combine(part_keep, part_send))
    with jax.named_scope("backward"):
        back_send = backward(down_sends, slope_send, BF)
        back_keep = backward(down_keeps, slope_keep, F32)
    with jax.named_scope("return_back"):
        back = reduce_y(combine(back_keep, back_send))
    with jax.named_scope("collect"):
        ready = call(
            pack_kernel,
            sds((packed, WIDE), BF),
            [VMEM] * 6,
            [pltpu.VMEM((packed, WIDE), BF)],
            flops=10**8,
            moved=10**6,
        )(*result, *back)
        mine = exchange(ready)
        theirs = swap_core(mine)
    with jax.named_scope("final"):
        layer_out, stream_grad = call(
            final_kernel,
            [sds((rows, width), BF)] * 2,
            [VMEM] * 7,
            [pltpu.VMEM((rows, width), F32)],
            flops=10**9,
            moved=4 * 10**6,
        )(mine, theirs, merge_high, merge_low, stream, gain, upstream)
    return (layer_out, stream_grad)


def solution(mesh):
    sizes = mesh.devices.shape
    shards = 4
    split = Mesh(
        mesh.devices.reshape(sizes[0] // shards, shards, sizes[1]), ("xz", "y", "core")
    )
    return jax.shard_map(
        per_device,
        mesh=split,
        in_specs=(
            P(("xz", "y"), "core"),
            P("core", None),
            P(("xz", "y", "core"), None),
            P(),
            P(("xz", "y"), None, "core"),
            P(("xz", "y"), "core", None),
            P(),
            P(),
            P(),
            P(("xz", "y", "core"), None),
        ),
        out_specs=(P(("xz", "y", "core"), None), P(("xz", "y", "core"), None)),
        check_vma=False,
    )
```

```python
import functools

import jax
import jax.numpy as jnp
from jax import lax
from jax.experimental import pallas as pl
from jax.experimental.pallas import tpu as pltpu
from jax.sharding import Mesh, PartitionSpec as P

SLOTS = 4
HALF = 2
BF = jnp.bfloat16
F32 = jnp.float32
I32 = jnp.int32
VMEM = pl.BlockSpec(memory_space=pltpu.VMEM)
SMEM = pl.BlockSpec(memory_space=pltpu.SMEM)
ANY = pl.BlockSpec(memory_space=pl.ANY)
WIDE = 896
PACK = 8


def mm(a, b):
    return jnp.dot(a, b, preferred_element_type=F32)


def mm_t(a, b):
    return lax.dot_general(a, b, (((1,), (1,)), ((), ())), preferred_element_type=F32)


def mm_a(a, b):
    return lax.dot_general(a, b, (((0,), (0,)), ((), ())), preferred_element_type=F32)


def cuts(size, step):
    return [(i, min(i + step, size)) for i in range(0, size, step)]


def iota(shape, dim):
    return lax.broadcasted_iota(I32, shape, dim)


def call(kernel, outs, in_specs, scratch=(), flops=0, moved=0, mib=16):
    return pl.pallas_call(
        kernel,
        out_shape=outs,
        in_specs=in_specs,
        out_specs=jax.tree.map(lambda _: VMEM, outs),
        scratch_shapes=list(scratch),
        compiler_params=pltpu.CompilerParams(vmem_limit_bytes=mib * 2**20),
        cost_estimate=pl.CostEstimate(flops=flops, bytes_accessed=moved, transcendentals=0),
    )


def open_kernel(ids, index, count, gate, context, weight, send, keep, pick_keep, pick_send, slots, ctx, w, sems):
    width = weight.shape[1]
    chunks = cuts(width, 512)
    load = pltpu.make_async_copy(context, ctx, sems.at[0])
    load.start()
    loads = []
    for i, (lo, hi) in enumerate(chunks):
        loads.append(pltpu.make_async_copy(weight.at[:, lo:hi], w.at[:, lo:hi], sems.at[i + 1]))
        loads[-1].start()
    core = ids[0]
    experts, capacity = index.shape
    packed = experts * PACK
    rows = send.shape[0]
    local = index[...] - ids[1]
    listed = iota((experts, capacity), 1) < count[...]
    mine = listed & (local >= 0) & (local < 2 * rows)
    upto = jnp.where(iota((capacity, capacity), 0) <= iota((capacity, capacity), 1), 1.0, 0.0)
    rank = mm(jnp.where(mine, 1.0, 0.0).astype(BF), upto.astype(BF))
    lane = iota((experts, 128), 1)
    at_row = jnp.zeros((experts, 128), F32)
    gates = jnp.zeros((experts, 128), F32)
    shifted = (local + 1).astype(F32)
    for slot in range(SLOTS):
        here = mine & (rank == slot + 1.0)
        row = jnp.sum(jnp.where(here, shifted, 0.0), axis=1, keepdims=True) - 1.0
        at_row = jnp.where(lane == slot, row, at_row)
        value = jnp.sum(jnp.where(here, gate[...], 0.0), axis=1, keepdims=True)
        gates = jnp.where(lane == slot, value, gates)
    at_row = at_row.astype(BF)
    gate_high = gates.astype(BF)
    slots[:experts, :] = at_row
    slots[experts : 2 * experts, :] = gate_high
    slots[2 * experts :, :] = (gates - gate_high.astype(F32)).astype(BF)
    down = mm(spread_of(experts), at_row)
    r_col = iota((packed, 128), 0) % PACK
    lane_id = iota((packed, 128), 1)
    k = iota((packed, 2 * rows), 1)
    r_wide = iota((packed, 2 * rows), 0) % PACK
    same_stream = (r_wide // 2) % 2 == k // rows
    patch = (core * rows + k % rows).astype(F32)
    for out, side in ((pick_keep, core), (pick_send, 1 - core)):
        slot = 2 * side + r_col % 2
        row = jnp.sum(jnp.where(lane_id == slot, down, 0.0), axis=1, keepdims=True)
        hot = same_stream & (row == patch)
        out[:, : 2 * rows] = jnp.where(hot & (r_wide < 4), 1.0, 0.0).astype(BF)
        out[:, 2 * rows :] = jnp.where(hot & (r_wide >= 4), 1.0, 0.0).astype(BF)
    load.wait()
    theirs = ctx[:, pl.ds(pl.multiple_of((1 - core) * rows, rows), rows)]
    ours = ctx[:, pl.ds(pl.multiple_of(core * rows, rows), rows)]
    for i, (lo, hi) in enumerate(chunks):
        loads[i].wait()
        send[:, lo:hi] = mm_a(theirs, w[:, lo:hi])
        keep[:, lo:hi] = mm_a(ours, w[:, lo:hi])


def spread_of(experts):
    shape = (experts * PACK, experts)
    return jnp.where(iota(shape, 0) // PACK == iota(shape, 1), 1.0, 0.0).astype(BF)


def merge_kernel(ids, slots, merge_high, merge_low):
    core = ids[0]
    experts = slots.shape[0] // 3
    packed = experts * PACK
    rows = merge_high.shape[0] // 4
    spread = spread_of(experts)
    across = [
        lax.dot_general(
            slots[i * experts : (i + 1) * experts, :],
            spread,
            (((0,), (1,)), ((), ())),
            preferred_element_type=F32,
        )
        for i in range(3)
    ]
    q = iota((128, packed), 1) % PACK
    sub = iota((128, packed), 0)
    own = (core * rows + iota((rows, packed), 0)).astype(F32)
    q_rows = iota((rows, packed), 1) % PACK
    for which, side in ((0, core), (1, 1 - core)):
        slot = 2 * side + q % 2
        row, high, low = (
            jnp.sum(jnp.where(sub == slot, part, 0.0), axis=0, keepdims=True) for part in across
        )
        hot = row == own
        for group in range(4):
            here = hot & (q_rows // 2 == group)
            at = (slice(group * rows, (group + 1) * rows), slice(which * packed, (which + 1) * packed))
            merge_high[at] = jnp.where(here, high, 0.0).astype(BF)
            merge_low[at] = jnp.where(here, low, 0.0).astype(BF)


def statistics(stream):
    mean = jnp.mean(stream, axis=-1, keepdims=True)
    centered = stream - mean
    variance = jnp.mean(centered * centered, axis=-1, keepdims=True)
    return centered, lax.rsqrt(variance + 1e-06)


def norm_kernel(att_keep, att_got, residual, gain, upstream, pick_keep, pick_send, stream, keep, send, both):
    rows, width = residual.shape
    total = residual[...].astype(F32) + (att_keep[...] + att_got[...])
    stream[...] = total
    centered, inverse = statistics(total)
    both[:rows, :] = (gain[...] * centered * inverse).astype(BF)
    both[rows:, :] = upstream[...]
    rest = width - WIDE
    for pick, out in ((pick_send, send), (pick_keep, keep)):
        first, second = pick[:, : 2 * rows], pick[:, 2 * rows :]
        out[:, :rest] = (mm(first, both[:, :rest]) + mm(second, both[:, WIDE:])).astype(BF)
        out[:, rest:] = mm(first, both[:, rest:WIDE]).astype(BF)


def place(packed):
    q = packed
    return (q % 64 // 2) * PACK + q // 64 * 2 + q % 2


def unpack_kernel(stream, got, *rest):
    out = rest[-1]
    n = got.shape[0]
    quarter = n // 4
    q = iota((2 * quarter, n), 0)
    q = q + (q // quarter + stream) * quarter
    order = jnp.where(place(q) == iota((2 * quarter, n), 1), 1.0, 0.0).astype(BF)
    flat = mm(order, got[...]).astype(BF)
    out[:, :WIDE] = flat[:quarter, :]
    out[:, WIDE:] = flat[quarter:, : out.shape[1] - WIDE]


def pack_kernel(own_r, one_r, two_r, own_b, one_b, two_b, out, flat):
    n = out.shape[0]
    quarter = n // 4
    rest = own_r.shape[1] - WIDE
    flat[2 * quarter :, rest:] = jnp.zeros((2 * quarter, WIDE - rest), BF)
    for stream, (own, one, two) in enumerate(((own_r, one_r, two_r), (own_b, one_b, two_b))):
        total = (own[...] + one[...].astype(F32) + two[...].astype(F32)).astype(BF)
        flat[stream * quarter : (stream + 1) * quarter, :] = total[:, :WIDE]
        flat[(2 + stream) * quarter : (3 + stream) * quarter, :rest] = total[:, WIDE:]
    order = jnp.where(iota((n, n), 0) == place(iota((n, n), 1)), 1.0, 0.0).astype(BF)
    out[...] = mm(order, flat[...]).astype(BF)


def forward_kernel(x0, x1, x2, x3, w1, w2, *rest):
    slope, part, x, hidden = rest[-4:]
    block = x0.shape[0]
    for i, ref in enumerate((x0, x1, x2, x3)):
        x[i * block : (i + 1) * block, :] = ref[...]
    for lo, hi in cuts(hidden.shape[1], 256):
        v = mm(x[...], w1[:, lo:hi])
        square = v * v
        t = jnp.tanh(0.7978845608 * v * (1.0 + 0.044715 * square))
        gate = 0.5 + 0.5 * t
        hidden[:, lo:hi] = (v * gate).astype(BF)
        slope[:, lo:hi] = gate + 0.5 * v * (1.0 - t * t) * (0.7978845608 * (1.0 + 0.134145 * square))
    for lo, hi in cuts(part.shape[1], 512):
        part[:, lo:hi] = mm(hidden[...], w2[:, lo:hi]).astype(part.dtype)


def backward_kernel(x0, x1, x2, x3, w1, w2, slope, *rest):
    part, x, grad = rest[-3:]
    block = x0.shape[0]
    for i, ref in enumerate((x0, x1, x2, x3)):
        x[i * block : (i + 1) * block, :] = ref[...]
    for lo, hi in cuts(grad.shape[1], 256):
        grad[:, lo:hi] = (mm_t(x[...], w2[lo:hi, :]) * slope[:, lo:hi]).astype(BF)
    for lo, hi in cuts(part.shape[1], 512):
        part[:, lo:hi] = mm_t(grad[...], w1[lo:hi, :]).astype(part.dtype)


def combine_kernel(keep, got, own, one, two, far):
    block = own.shape[0]
    for i, out in enumerate((own, one, two, far)):
        at = slice(i * block, (i + 1) * block)
        out[...] = (keep[at, :] + got[at, :].astype(F32)).astype(out.dtype)


def add_kernel(a, b, out):
    out[...] = (a[...].astype(F32) + b[...].astype(F32)).astype(BF)


def final_kernel(mine, theirs, merge_high, merge_low, stream, gain, upstream, layer_out, stream_grad, back):
    rows, width = stream.shape
    n = mine.shape[0]
    rest = width - WIDE
    total = stream[...]
    centered, inverse = statistics(total)
    x_hat = centered * inverse
    for group in range(4):
        at = slice(group * rows, (group + 1) * rows)
        summed = mm(merge_high[at, :n], mine[...]) + mm(merge_high[at, n:], theirs[...])
        summed += mm(merge_low[at, :n], mine[...]) + mm(merge_low[at, n:], theirs[...])
        cols = slice(0, WIDE) if group < 2 else slice(WIDE, width)
        summed = summed if group < 2 else summed[:, :rest]
        if group % 2 == 0:
            layer_out[:, cols] = (total[:, cols] + summed).astype(BF)
        else:
            back[:, cols] = summed
    scaled = gain[...] * back[...]
    mean = jnp.mean(scaled, axis=-1, keepdims=True)
    along = jnp.mean(scaled * x_hat, axis=-1, keepdims=True)
    pulled = inverse * (scaled - mean - x_hat * along)
    stream_grad[...] = (upstream[...].astype(F32) + pulled).astype(BF)


def per_device(
    context,
    out_weight,
    residual,
    norm_gain,
    expert_in,
    expert_out,
    patch_index,
    patch_count,
    gate_value,
    upstream,
):
    rows, width = residual.shape
    experts, capacity = patch_index.shape
    shards = lax.axis_size("y")
    packed = experts * PACK
    block = experts * HALF
    units = expert_in.shape[2]
    sds = jax.ShapeDtypeStruct
    core = lax.axis_index("core")
    index = lax.axis_index("xz") * shards + lax.axis_index("y")
    ids = jnp.stack([core, index * (2 * rows)]).astype(I32)
    gain = norm_gain.reshape(1, width)

    def swap_core(x):
        return lax.ppermute(x, "core", [(0, 1), (1, 0)])

    def ring(x, way):
        pairs = []
        for y in range(shards):
            for c in range(2):
                step = way if c == 0 else -way
                pairs.append((y * 2 + c, (y + step) % shards * 2 + c))
        return lax.ppermute(x, ("y", "core"), pairs)

    def exchange(x):
        got = lax.all_to_all(
            x.reshape(experts, PACK, WIDE), "xz", split_axis=0, concat_axis=0, tiled=True
        )
        return got.reshape(packed, WIDE)

    with jax.named_scope("open"):
        att_send, att_keep, pick_keep, pick_send, slots = call(
            open_kernel,
            [sds((rows, width), F32)] * 2 + [sds((packed, 4 * rows), BF)] * 2 + [sds((3 * experts, 128), BF)],
            [SMEM] + [VMEM] * 3 + [ANY] * 2,
            [
                pltpu.VMEM((context.shape[1], 2 * rows), BF),
                pltpu.VMEM(out_weight.shape, BF),
                pltpu.SemaphoreType.DMA((1 + len(cuts(width, 512)),)),
            ],
            flops=4 * rows * width * context.shape[1],
            moved=5 * 10**6,
        )(ids, patch_index, patch_count.reshape(experts, 1), gate_value, context.T, out_weight)
        att_got = swap_core(att_send)
    with jax.named_scope("merge"):
        merge_high, merge_low = call(
            merge_kernel,
            [sds((4 * rows, 2 * packed), BF)] * 2,
            [SMEM, VMEM],
            flops=10**8,
            moved=10**6,
        )(ids, slots)
    with jax.named_scope("norm"):
        stream, keep, send = call(
            norm_kernel,
            [sds((rows, width), F32)] + [sds((packed, WIDE), BF)] * 2,
            [VMEM] * 7,
            [pltpu.VMEM((2 * rows, width), BF)],
            flops=10**9,
            moved=3 * 10**6,
        )(att_keep, att_got, residual, gain, upstream, pick_keep, pick_send)
    with jax.named_scope("dispatch"):
        got = exchange(keep + swap_core(send))

    def unpack(stream, *after):
        return call(
            functools.partial(unpack_kernel, stream),
            sds((block, width), BF),
            [VMEM] + [ANY] * len(after),
            flops=10**8,
            moved=10**6,
        )(got, *after)

    def gather_y(own):
        one = ring(own, 1)
        two = ring(own, -1)
        far = ring(one, 1)
        keeps = [own, one, two, far]
        return keeps, [swap_core(x) for x in keeps]

    def combine(keep_part, send_part):
        return call(
            combine_kernel,
            [sds((block, width), F32)] * 2 + [sds((block, width), BF)] * 2,
            [VMEM] * 2,
            flops=10**6,
            moved=4 * 10**6,
        )(keep_part, swap_core(send_part))

    def reduce_y(parts):
        own, one, two, far = parts
        from_far = ring(far, -1)
        from_two = ring(two, 1)
        one = call(add_kernel, sds((block, width), BF), [VMEM] * 2, flops=10**5, moved=10**6)(one, from_far)
        return (own, ring(one, -1), from_two), (far, one, from_two)

    weight_in = expert_in[0]
    weight_out = expert_out[0]
    tall = shards * block
    flops = 16 * tall * width * units

    def forward(xs, kind, *after):
        return call(
            forward_kernel,
            [sds((tall, units), F32), sds((tall, width), kind)],
            [VMEM] * 6 + [ANY] * len(after),
            [pltpu.VMEM((tall, width), BF), pltpu.VMEM((tall, units), BF)],
            flops=flops,
            moved=10**7,
            mib=24,
        )(*xs, weight_in, weight_out, *after)

    def backward(xs, slope, kind, *after):
        return call(
            backward_kernel,
            sds((tall, width), kind),
            [VMEM] * 7 + [ANY] * len(after),
            [pltpu.VMEM((tall, width), BF), pltpu.VMEM((tall, units), BF)],
            flops=flops,
            moved=10**7,
            mib=24,
        )(*xs, weight_in, weight_out, slope, *after)

    with jax.named_scope("gather_normed"):
        keeps, sends = gather_y(unpack(0))
    with jax.named_scope("gather_down"):
        down_keeps, down_sends = gather_y(unpack(1, keeps[1], keeps[2]))
    with jax.named_scope("forward"):
        slope_send, part_send = forward(sends, BF)
        slope_keep, part_keep = forward(keeps, F32, down_keeps[1], down_keeps[2])
    with jax.named_scope("return_result"):
        result, passed = reduce_y(combine(part_keep, part_send))
    with jax.named_scope("backward"):
        back_send = backward(down_sends, slope_send, BF, passed[0])
        back_keep = backward(down_keeps, slope_keep, F32, *passed[1:])
    with jax.named_scope("return_back"):
        back, _ = reduce_y(combine(back_keep, back_send))
    with jax.named_scope("collect"):
        ready = call(
            pack_kernel,
            sds((packed, WIDE), BF),
            [VMEM] * 6,
            [pltpu.VMEM((packed, WIDE), BF)],
            flops=10**8,
            moved=10**6,
        )(*result, *back)
        mine = exchange(ready)
        theirs = swap_core(mine)
    with jax.named_scope("final"):
        layer_out, stream_grad = call(
            final_kernel,
            [sds((rows, width), BF)] * 2,
            [VMEM] * 7,
            [pltpu.VMEM((rows, width), F32)],
            flops=10**9,
            moved=4 * 10**6,
        )(mine, theirs, merge_high, merge_low, stream, gain, upstream)
    return (layer_out, stream_grad)


def solution(mesh):
    sizes = mesh.devices.shape
    shards = 4
    split = Mesh(
        mesh.devices.reshape(sizes[0] // shards, shards, sizes[1]), ("xz", "y", "core")
    )
    return jax.shard_map(
        per_device,
        mesh=split,
        in_specs=(
            P(("xz", "y"), "core"),
            P("core", None),
            P(("xz", "y", "core"), None),
            P(),
            P(("xz", "y"), None, "core"),
            P(("xz", "y"), "core", None),
            P(),
            P(),
            P(),
            P(("xz", "y", "core"), None),
        ),
        out_specs=(P(("xz", "y", "core"), None), P(("xz", "y", "core"), None)),
        check_vma=False,
    )
```

```python
import jax
import jax.numpy as jnp
from jax import lax
from jax.experimental import pallas as pl
from jax.experimental.pallas import tpu as pltpu
from jax.sharding import Mesh, PartitionSpec as P

SLOTS = 4
HALF = 2
BF = jnp.bfloat16
F32 = jnp.float32
I32 = jnp.int32
VMEM = pl.BlockSpec(memory_space=pltpu.VMEM)
SMEM = pl.BlockSpec(memory_space=pltpu.SMEM)
ANY = pl.BlockSpec(memory_space=pl.ANY)
WIDE = 896
PACK = 8
PARTS = ((0, 512), (512, 896), (896, 1280), (1280, 1664))


def mm(a, b):
    return jnp.dot(a, b, preferred_element_type=F32)


def mm_t(a, b):
    return lax.dot_general(a, b, (((1,), (1,)), ((), ())), preferred_element_type=F32)


def mm_a(a, b):
    return lax.dot_general(a, b, (((0,), (0,)), ((), ())), preferred_element_type=F32)


def cuts(size, step):
    return [(i, min(i + step, size)) for i in range(0, size, step)]


def iota(shape, dim):
    return lax.broadcasted_iota(I32, shape, dim)


def call(kernel, outs, in_specs, scratch=(), flops=0, moved=0, mib=16):
    return pl.pallas_call(
        kernel,
        out_shape=outs,
        in_specs=in_specs,
        out_specs=jax.tree.map(lambda _: VMEM, outs),
        scratch_shapes=list(scratch),
        compiler_params=pltpu.CompilerParams(vmem_limit_bytes=mib * 2**20),
        cost_estimate=pl.CostEstimate(flops=flops, bytes_accessed=moved, transcendentals=0),
    )


def select(hot, rows, out):
    part = iota(hot.shape, 0) % PACK // 2
    picks = [jnp.where(part == i, hot[...], 0.0).astype(BF) for i in range(len(PARTS))]
    low = PARTS[-1][1] - PARTS[-1][0]
    total = mm(picks[0], rows[:, :low])
    for pick, (lo, hi) in zip(picks[1:], PARTS[1:]):
        total += mm(pick, rows[:, lo:hi])
    out[:, :low] = total.astype(BF)
    out[:, low:] = mm(picks[0], rows[:, low : PARTS[0][1]]).astype(BF)


def open_kernel(ids, index, count, gate, upstream, hot_keep, hot_send, slots, keep, send):
    core = ids[0]
    experts, capacity = index.shape
    packed = experts * PACK
    rows = upstream.shape[0]
    local = index[...] - ids[1]
    listed = iota((experts, capacity), 1) < count[...]
    mine = listed & (local >= 0) & (local < 2 * rows)
    upto = jnp.where(iota((capacity, capacity), 0) <= iota((capacity, capacity), 1), 1.0, 0.0)
    rank = mm(jnp.where(mine, 1.0, 0.0).astype(BF), upto.astype(BF))
    lane = iota((experts, 128), 1)
    at_row = jnp.zeros((experts, 128), F32)
    gates = jnp.zeros((experts, 128), F32)
    shifted = (local + 1).astype(F32)
    for slot in range(SLOTS):
        here = mine & (rank == slot + 1.0)
        row = jnp.sum(jnp.where(here, shifted, 0.0), axis=1, keepdims=True) - 1.0
        at_row = jnp.where(lane == slot, row, at_row)
        value = jnp.sum(jnp.where(here, gate[...], 0.0), axis=1, keepdims=True)
        gates = jnp.where(lane == slot, value, gates)
    at_row = at_row.astype(BF)
    gate_high = gates.astype(BF)
    slots[:experts, :] = at_row
    slots[experts : 2 * experts, :] = gate_high
    slots[2 * experts :, :] = (gates - gate_high.astype(F32)).astype(BF)
    down = mm(spread_of(experts), at_row)
    r = iota((packed, 128), 0) % PACK
    lane_id = iota((packed, 128), 1)
    patch = (core * rows + iota((packed, rows), 1)).astype(F32)
    for hot, out, side in ((hot_send, send, 1 - core), (hot_keep, keep, core)):
        row = jnp.sum(jnp.where(lane_id == 2 * side + r % 2, down, 0.0), axis=1, keepdims=True)
        hot[...] = jnp.where(row == patch, 1.0, 0.0).astype(BF)
        select(hot, upstream, out)


def attend_kernel(ids, context, weight, after, send, keep, w, sems):
    chunks = cuts(weight.shape[1], 512)
    loads = []
    for i, (lo, hi) in enumerate(chunks):
        loads.append(pltpu.make_async_copy(weight.at[:, lo:hi], w.at[:, lo:hi], sems.at[i]))
        loads[-1].start()
    core = ids[0]
    rows = send.shape[0]
    theirs = context[:, pl.ds(pl.multiple_of((1 - core) * rows, rows), rows)]
    ours = context[:, pl.ds(pl.multiple_of(core * rows, rows), rows)]
    for i, (lo, hi) in enumerate(chunks):
        loads[i].wait()
        send[:, lo:hi] = mm_a(theirs, w[:, lo:hi])
        keep[:, lo:hi] = mm_a(ours, w[:, lo:hi])


def spread_of(experts):
    shape = (experts * PACK, experts)
    return jnp.where(iota(shape, 0) // PACK == iota(shape, 1), 1.0, 0.0).astype(BF)


def merge_kernel(ids, slots, merge_high, merge_low):
    core = ids[0]
    experts = slots.shape[0] // 3
    packed = experts * PACK
    rows = merge_high.shape[0] // 4
    spread = spread_of(experts)
    across = [
        lax.dot_general(
            slots[i * experts : (i + 1) * experts, :],
            spread,
            (((0,), (1,)), ((), ())),
            preferred_element_type=F32,
        )
        for i in range(3)
    ]
    q = iota((128, packed), 1) % PACK
    sub = iota((128, packed), 0)
    own = (core * rows + iota((rows, packed), 0)).astype(F32)
    q_rows = iota((rows, packed), 1) % PACK
    for which, side in ((0, core), (1, 1 - core)):
        slot = 2 * side + q % 2
        row, high, low = (
            jnp.sum(jnp.where(sub == slot, part, 0.0), axis=0, keepdims=True) for part in across
        )
        hot = row == own
        for group in range(4):
            here = hot & (q_rows // 2 == group)
            at = (slice(group * rows, (group + 1) * rows), slice(which * packed, (which + 1) * packed))
            merge_high[at] = jnp.where(here, high, 0.0).astype(BF)
            merge_low[at] = jnp.where(here, low, 0.0).astype(BF)


def statistics(stream):
    mean = jnp.mean(stream, axis=-1, keepdims=True)
    centered = stream - mean
    variance = jnp.mean(centered * centered, axis=-1, keepdims=True)
    return centered, lax.rsqrt(variance + 1e-06)


def norm_kernel(att_keep, att_got, residual, gain, hot_keep, hot_send, stream, keep, send, normed):
    total = residual[...].astype(F32) + (att_keep[...] + att_got[...])
    stream[...] = total
    centered, inverse = statistics(total)
    normed[...] = (gain[...] * centered * inverse).astype(BF)
    select(hot_send, normed, send)
    select(hot_keep, normed, keep)


def unpack_kernel(got, *rest):
    out = rest[-1]
    n = got.shape[0]
    q = iota((n // 4, n), 0)
    for i, (lo, hi) in enumerate(PARTS):
        order = jnp.where(q // 2 * PACK + i * 2 + q % 2 == iota((n // 4, n), 1), 1.0, 0.0).astype(BF)
        out[:, lo:hi] = mm(order, got[:, : hi - lo]).astype(BF)


def stack_kernel(*refs):
    block = refs[0].shape[0]
    for i, ref in enumerate(refs[:-1]):
        refs[-1][i * block : (i + 1) * block, :] = ref[...]


def place(packed):
    q = packed
    return (q % 64 // 2) * PACK + q // 64 * 2 + q % 2


def pack_kernel(own, one, two, out, flat):
    n = out.shape[0]
    quarter = n // 4
    rest = own.shape[1] - WIDE
    total = (own[...] + one[...].astype(F32) + two[...].astype(F32)).astype(BF)
    flat[: 2 * quarter, :] = total[:, :WIDE]
    flat[2 * quarter :, :rest] = total[:, WIDE:]
    flat[2 * quarter :, rest:] = jnp.zeros((2 * quarter, WIDE - rest), BF)
    order = jnp.where(iota((n, n), 0) == place(iota((n, n), 1)), 1.0, 0.0).astype(BF)
    out[...] = mm(order, flat[...]).astype(BF)


def lift_kernel(u, w2, out):
    for lo, hi in cuts(out.shape[1], 256):
        out[:, lo:hi] = mm_t(u[...], w2[lo:hi, :])


def expert(x, lifted, w1, w2, hidden, grad, store):
    for lo, hi in cuts(hidden.shape[1], 256):
        v = mm(x[...], w1[:, lo:hi])
        square = v * v
        t = jnp.tanh(0.7978845608 * v * (1.0 + 0.044715 * square))
        gate = 0.5 + 0.5 * t
        hidden[:, lo:hi] = (v * gate).astype(BF)
        slope = gate + 0.5 * v * (1.0 - t * t) * (0.7978845608 * (1.0 + 0.134145 * square))
        grad[:, lo:hi] = (lifted(lo, hi) * slope).astype(BF)
    for lo, hi in cuts(w2.shape[1], 512):
        store(0, lo, hi, mm(hidden[...], w2[:, lo:hi]))
        store(1, lo, hi, mm_t(grad[...], w1[lo:hi, :]))


def near_kernel(x, lifted, w1, w2, part, hidden, grad):
    rows = x.shape[0]

    def store(stream, lo, hi, value):
        part[stream * rows : (stream + 1) * rows, lo:hi] = value.astype(part.dtype)

    expert(x, lambda lo, hi: lifted[:rows, lo:hi], w1, w2, hidden, grad, store)


def far_kernel(x_keep, x_send, lifted_keep, lifted_send, w1, w2, keep, send, x, hidden, grad, lifted):
    rows = x_keep.shape[0]
    x[:rows, :] = x_keep[...]
    x[rows:, :] = x_send[...]
    lifted[:rows, :] = lifted_keep[-rows:, :]
    lifted[rows:, :] = lifted_send[-rows:, :]

    def store(stream, lo, hi, value):
        at = slice(stream * rows, (stream + 1) * rows)
        keep[at, lo:hi] = value[:rows, :]
        send[at, lo:hi] = value[rows:, :].astype(send.dtype)

    expert(x, lambda lo, hi: lifted[:, lo:hi], w1, w2, hidden, grad, store)


def combine_kernel(keep, got, *outs):
    block = outs[0].shape[0] // 2
    for stream in range(2):
        for i, out in enumerate(outs):
            lo = (stream * len(outs) + i) * block
            at = slice(lo, lo + block)
            total = keep[at, :] + got[at, :].astype(F32)
            out[stream * block : (stream + 1) * block, :] = total.astype(out.dtype)


def add_kernel(a, b, out):
    out[...] = (a[...].astype(F32) + b[...].astype(F32)).astype(BF)


def final_kernel(mine, theirs, merge_high, merge_low, stream, gain, upstream, layer_out, stream_grad, back):
    rows, width = stream.shape
    n = mine.shape[0]
    rest = width - WIDE
    total = stream[...]
    centered, inverse = statistics(total)
    x_hat = centered * inverse
    for group in range(4):
        at = slice(group * rows, (group + 1) * rows)
        summed = mm(merge_high[at, :n], mine[...]) + mm(merge_high[at, n:], theirs[...])
        summed += mm(merge_low[at, :n], mine[...]) + mm(merge_low[at, n:], theirs[...])
        cols = slice(0, WIDE) if group < 2 else slice(WIDE, width)
        summed = summed if group < 2 else summed[:, :rest]
        if group % 2 == 0:
            layer_out[:, cols] = (total[:, cols] + summed).astype(BF)
        else:
            back[:, cols] = summed
    scaled = gain[...] * back[...]
    mean = jnp.mean(scaled, axis=-1, keepdims=True)
    along = jnp.mean(scaled * x_hat, axis=-1, keepdims=True)
    pulled = inverse * (scaled - mean - x_hat * along)
    stream_grad[...] = (upstream[...].astype(F32) + pulled).astype(BF)


def per_device(
    context,
    out_weight,
    residual,
    norm_gain,
    expert_in,
    expert_out,
    patch_index,
    patch_count,
    gate_value,
    upstream,
):
    rows, width = residual.shape
    experts, capacity = patch_index.shape
    shards = lax.axis_size("y")
    packed = experts * PACK
    block = experts * HALF
    units = expert_in.shape[2]
    sds = jax.ShapeDtypeStruct
    core = lax.axis_index("core")
    index = lax.axis_index("xz") * shards + lax.axis_index("y")
    ids = jnp.stack([core, index * (2 * rows)]).astype(I32)
    gain = norm_gain.reshape(1, width)

    def swap_core(x):
        return lax.ppermute(x, "core", [(0, 1), (1, 0)])

    def ring(x, way):
        pairs = []
        for y in range(shards):
            for c in range(2):
                step = way if c == 0 else -way
                pairs.append((y * 2 + c, (y + step) % shards * 2 + c))
        return lax.ppermute(x, ("y", "core"), pairs)

    def exchange(x):
        got = lax.all_to_all(
            x.reshape(experts, PACK, x.shape[1]), "xz", split_axis=0, concat_axis=0, tiled=True
        )
        return got.reshape(x.shape)

    weight_in = expert_in[0]
    weight_out = expert_out[0]
    tall = shards * block
    thin = PARTS[0][1]
    pack_sds = sds((packed, thin), BF)

    def unpack(got, *after):
        out = sds((block, width), BF)
        specs = [VMEM] + [ANY] * len(after)
        return call(unpack_kernel, out, specs, flops=10**8, moved=10**6)(got, *after)

    def stack(*xs):
        out = sds((block * len(xs), width), BF)
        return call(stack_kernel, out, [VMEM] * len(xs), flops=10**5, moved=10**6)(*xs)

    with jax.named_scope("open"):
        hot_keep, hot_send, slots, down_keep, down_send = call(
            open_kernel,
            [sds((packed, rows), BF)] * 2 + [sds((3 * experts, 128), BF)] + [pack_sds] * 2,
            [SMEM] + [VMEM] * 4,
            flops=10**9,
            moved=10**6,
            mib=56,
        )(ids, patch_index, patch_count.reshape(experts, 1), gate_value, upstream)
        down_packed = down_keep + swap_core(down_send)
    with jax.named_scope("attend"):
        att_send, att_keep = call(
            attend_kernel,
            [sds((rows, width), F32)] * 2,
            [SMEM, VMEM, ANY, ANY],
            [pltpu.VMEM(out_weight.shape, BF), pltpu.SemaphoreType.DMA((len(cuts(width, 512)),))],
            flops=4 * rows * width * context.shape[1],
            moved=5 * 10**6,
            mib=56,
        )(ids, context.T, out_weight, slots)
        att_got = swap_core(att_send)
    with jax.named_scope("norm"):
        stream, keep, send = call(
            norm_kernel,
            [sds((rows, width), F32)] + [pack_sds] * 2,
            [VMEM] * 6,
            [pltpu.VMEM((rows, width), BF)],
            flops=10**9,
            moved=3 * 10**6,
        )(att_keep, att_got, residual, gain, hot_keep, hot_send)
    with jax.named_scope("dispatch_normed"):
        packed_rows = keep + swap_core(send)
        own = unpack(exchange(packed_rows))
    with jax.named_scope("dispatch_down"):
        down_rows = unpack(exchange(down_packed), packed_rows)
    with jax.named_scope("merge"):
        merge_high, merge_low = call(
            merge_kernel,
            [sds((4 * rows, 2 * packed), BF)] * 2,
            [SMEM, VMEM],
            flops=10**8,
            moved=10**6,
        )(ids, slots)

    def lift(u):
        return call(
            lift_kernel,
            sds((tall, units), F32),
            [VMEM] * 2,
            flops=4 * tall * width * units,
            moved=6 * 10**6,
            mib=16,
        )(u, weight_out)

    def near_part(x, lifted, kind):
        tall = x.shape[0]
        return call(
            near_kernel,
            sds((2 * tall, width), kind),
            [VMEM] * 4,
            [pltpu.VMEM((tall, units), BF)] * 2,
            flops=20 * tall * width * units,
            moved=10**7,
            mib=20,
        )(x, lifted, weight_in, weight_out)

    with jax.named_scope("gather_down"):
        down_one = ring(down_rows, 1)
        down_two = ring(down_rows, -1)
        down_far = ring(down_one, 1)
        downs = stack(down_rows, down_one, down_two, down_far)
        lifted_send = lift(swap_core(downs))
        lifted_keep = lift(downs)
    with jax.named_scope("gather_normed"):
        one = ring(own, 1)
        two = ring(own, -1)
        far = ring(one, 1)
        near = stack(own, one, two)
        near_send = swap_core(near)
        far_send = swap_core(far)
    pair = (2 * block, width)
    with jax.named_scope("experts"):
        near_keep = near_part(near, lifted_keep, F32)
        near_got = swap_core(near_part(near_send, lifted_send, BF))
        far_keep, far_out = call(
            far_kernel,
            [sds(pair, F32), sds(pair, BF)],
            [VMEM] * 6,
            [pltpu.VMEM(pair, BF)]
            + [pltpu.VMEM((2 * block, units), BF)] * 2
            + [pltpu.VMEM((2 * block, units), F32)],
            flops=40 * block * width * units,
            moved=10**7,
            mib=20,
        )(far, far_send, lifted_keep, lifted_send, weight_in, weight_out)
        far_got = swap_core(far_out)
    with jax.named_scope("reduce"):

        def combine(keep, got, *kinds):
            outs = [sds(pair, kind) for kind in kinds]
            return call(combine_kernel, outs, [VMEM] * 2, flops=10**6, moved=10**6)(keep, got)

        own_sum, one_sum, two_sum = combine(near_keep, near_got, F32, F32, BF)
        (far_sum,) = combine(far_keep, far_got, BF)
        from_far = ring(far_sum, -1)
        from_two = ring(two_sum, 1)
        one_sum = call(add_kernel, sds(pair, BF), [VMEM] * 2, flops=10**5, moved=10**6)(one_sum, from_far)
        from_one = ring(one_sum, -1)
    with jax.named_scope("collect"):
        ready = call(
            pack_kernel,
            sds((packed, WIDE), BF),
            [VMEM] * 3,
            [pltpu.VMEM((packed, WIDE), BF)],
            flops=10**8,
            moved=10**6,
        )(own_sum, from_one, from_two)
        mine = exchange(ready)
        theirs = swap_core(mine)
    with jax.named_scope("final"):
        layer_out, stream_grad = call(
            final_kernel,
            [sds((rows, width), BF)] * 2,
            [VMEM] * 7,
            [pltpu.VMEM((rows, width), F32)],
            flops=10**9,
            moved=4 * 10**6,
        )(mine, theirs, merge_high, merge_low, stream, gain, upstream)
    return (layer_out, stream_grad)


def solution(mesh):
    sizes = mesh.devices.shape
    shards = 4
    split = Mesh(
        mesh.devices.reshape(sizes[0] // shards, shards, sizes[1]), ("xz", "y", "core")
    )
    return jax.shard_map(
        per_device,
        mesh=split,
        in_specs=(
            P(("xz", "y"), "core"),
            P("core", None),
            P(("xz", "y", "core"), None),
            P(),
            P(("xz", "y"), None, "core"),
            P(("xz", "y"), "core", None),
            P(),
            P(),
            P(),
            P(("xz", "y", "core"), None),
        ),
        out_specs=(P(("xz", "y", "core"), None), P(("xz", "y", "core"), None)),
        check_vma=False,
    )
```

```python
import jax
import jax.numpy as jnp
from jax import lax
from jax.experimental import pallas as pl
from jax.experimental.pallas import tpu as pltpu
from jax.sharding import Mesh, PartitionSpec as P

SLOTS = 4
HALF = 2
BF = jnp.bfloat16
F32 = jnp.float32
I32 = jnp.int32
VMEM = pl.BlockSpec(memory_space=pltpu.VMEM)
SMEM = pl.BlockSpec(memory_space=pltpu.SMEM)
ANY = pl.BlockSpec(memory_space=pl.ANY)
WIDE = 896
PACK = 8


def mm(a, b):
    return jnp.dot(a, b, preferred_element_type=F32)


def mm_t(a, b):
    return lax.dot_general(a, b, (((1,), (1,)), ((), ())), preferred_element_type=F32)


def mm_a(a, b):
    return lax.dot_general(a, b, (((0,), (0,)), ((), ())), preferred_element_type=F32)


def cuts(size, step):
    return [(i, min(i + step, size)) for i in range(0, size, step)]


def iota(shape, dim):
    return lax.broadcasted_iota(I32, shape, dim)


def call(kernel, outs, in_specs, scratch=(), flops=0, moved=0, mib=16):
    return pl.pallas_call(
        kernel,
        out_shape=outs,
        in_specs=in_specs,
        out_specs=jax.tree.map(lambda _: VMEM, outs),
        scratch_shapes=list(scratch),
        compiler_params=pltpu.CompilerParams(vmem_limit_bytes=mib * 2**20),
        cost_estimate=pl.CostEstimate(flops=flops, bytes_accessed=moved, transcendentals=0),
    )


def routing_kernel(ids, index, count, gate, pick_keep, pick_send, slots):
    core = ids[0]
    experts, capacity = index.shape
    packed = experts * PACK
    rows = pick_keep.shape[1] // 4
    local = index[...] - ids[1]
    diagonal = iota((experts, experts), 0) == iota((experts, experts), 1)
    counts = jnp.sum(jnp.where(diagonal, count[...].astype(F32), 0.0), axis=1, keepdims=True)
    listed = iota((experts, capacity), 1).astype(F32) < counts
    mine = listed & (local >= 0) & (local < 2 * rows)
    upto = jnp.where(iota((capacity, capacity), 0) <= iota((capacity, capacity), 1), 1.0, 0.0)
    rank = mm(jnp.where(mine, 1.0, 0.0).astype(BF), upto.astype(BF))
    lane = iota((experts, 128), 1)
    at_row = jnp.zeros((experts, 128), F32)
    gates = jnp.zeros((experts, 128), F32)
    shifted = (local + 1).astype(F32)
    for slot in range(SLOTS):
        here = mine & (rank == slot + 1.0)
        row = jnp.sum(jnp.where(here, shifted, 0.0), axis=1, keepdims=True) - 1.0
        at_row = jnp.where(lane == slot, row, at_row)
        value = jnp.sum(jnp.where(here, gate[...], 0.0), axis=1, keepdims=True)
        gates = jnp.where(lane == slot, value, gates)
    at_row = at_row.astype(BF)
    gate_high = gates.astype(BF)
    slots[:experts, :] = at_row
    slots[experts : 2 * experts, :] = gate_high
    slots[2 * experts :, :] = (gates - gate_high.astype(F32)).astype(BF)
    down = mm(spread_of(experts), at_row)
    r_col = iota((packed, 128), 0) % PACK
    lane_id = iota((packed, 128), 1)
    k = iota((packed, 2 * rows), 1)
    r_wide = iota((packed, 2 * rows), 0) % PACK
    same_stream = (r_wide // 2) % 2 == k // rows
    patch = (core * rows + k % rows).astype(F32)
    for out, side in ((pick_keep, core), (pick_send, 1 - core)):
        slot = 2 * side + r_col % 2
        row = jnp.sum(jnp.where(lane_id == slot, down, 0.0), axis=1, keepdims=True)
        hot = same_stream & (row == patch)
        out[:, : 2 * rows] = jnp.where(hot & (r_wide < 4), 1.0, 0.0).astype(BF)
        out[:, 2 * rows :] = jnp.where(hot & (r_wide >= 4), 1.0, 0.0).astype(BF)


def attend_kernel(ids, context, weight, after, send, keep):
    core = ids[0]
    rows = send.shape[0]
    for out, at in ((send, 1 - core), (keep, core)):
        block = context[:, pl.ds(pl.multiple_of(at * rows, rows), rows)]
        for lo, hi in cuts(out.shape[1], 512):
            out[:, lo:hi] = mm_a(block, weight[:, lo:hi])


def spread_of(experts):
    shape = (experts * PACK, experts)
    return jnp.where(iota(shape, 0) // PACK == iota(shape, 1), 1.0, 0.0).astype(BF)


def merge_kernel(ids, slots, merge_high, merge_low):
    core = ids[0]
    experts = slots.shape[0] // 3
    packed = experts * PACK
    rows = merge_high.shape[0] // 4
    spread = spread_of(experts)
    across = [
        lax.dot_general(
            slots[i * experts : (i + 1) * experts, :],
            spread,
            (((0,), (1,)), ((), ())),
            preferred_element_type=F32,
        )
        for i in range(3)
    ]
    q = iota((128, packed), 1) % PACK
    sub = iota((128, packed), 0)
    own = (core * rows + iota((rows, packed), 0)).astype(F32)
    q_rows = iota((rows, packed), 1) % PACK
    for which, side in ((0, core), (1, 1 - core)):
        slot = 2 * side + q % 2
        row, high, low = (
            jnp.sum(jnp.where(sub == slot, part, 0.0), axis=0, keepdims=True) for part in across
        )
        hot = row == own
        for group in range(4):
            here = hot & (q_rows // 2 == group)
            at = (slice(group * rows, (group + 1) * rows), slice(which * packed, (which + 1) * packed))
            merge_high[at] = jnp.where(here, high, 0.0).astype(BF)
            merge_low[at] = jnp.where(here, low, 0.0).astype(BF)


def statistics(stream):
    mean = jnp.mean(stream, axis=-1, keepdims=True)
    centered = stream - mean
    variance = jnp.mean(centered * centered, axis=-1, keepdims=True)
    return centered, lax.rsqrt(variance + 1e-06)


def norm_kernel(att_keep, att_got, residual, gain, upstream, pick_keep, pick_send, stream, keep, send, both):
    rows, width = residual.shape
    total = residual[...].astype(F32) + (att_keep[...] + att_got[...])
    stream[...] = total
    centered, inverse = statistics(total)
    both[:rows, :] = (gain[...] * centered * inverse).astype(BF)
    both[rows:, :] = upstream[...]
    rest = width - WIDE
    for pick, out in ((pick_send, send), (pick_keep, keep)):
        first, second = pick[:, : 2 * rows], pick[:, 2 * rows :]
        out[:, :rest] = (mm(first, both[:, :rest]) + mm(second, both[:, WIDE:])).astype(BF)
        out[:, rest:] = mm(first, both[:, rest:WIDE]).astype(BF)


def place(packed):
    q = packed
    return (q % 64 // 2) * PACK + q // 64 * 2 + q % 2


def unpack_kernel(got, out):
    n = got.shape[0]
    half = n // 2
    order = jnp.where(place(iota((n, n), 0)) == iota((n, n), 1), 1.0, 0.0).astype(BF)
    flat = mm(order, got[...]).astype(BF)
    out[:, :WIDE] = flat[:half, :]
    out[:, WIDE:] = flat[half:, : out.shape[1] - WIDE]


def stack_kernel(*refs):
    out = refs[-1]
    block = refs[0].shape[0] // 2
    for stream in range(2):
        for i, ref in enumerate(refs[:-1]):
            lo = (stream * (len(refs) - 1) + i) * block
            out[lo : lo + block, :] = ref[stream * block : (stream + 1) * block, :]


def pack_kernel(own, one, two, out, flat):
    n = out.shape[0]
    quarter = n // 4
    rest = own.shape[1] - WIDE
    total = (own[...] + one[...].astype(F32) + two[...].astype(F32)).astype(BF)
    flat[: 2 * quarter, :] = total[:, :WIDE]
    flat[2 * quarter :, :rest] = total[:, WIDE:]
    flat[2 * quarter :, rest:] = jnp.zeros((2 * quarter, WIDE - rest), BF)
    order = jnp.where(iota((n, n), 0) == place(iota((n, n), 1)), 1.0, 0.0).astype(BF)
    out[...] = mm(order, flat[...]).astype(BF)


def expert(x, u, w1, w2, hidden, grad, store):
    for lo, hi in cuts(hidden.shape[1], 256):
        v = mm(x, w1[:, lo:hi])
        square = v * v
        t = jnp.tanh(0.7978845608 * v * (1.0 + 0.044715 * square))
        gate = 0.5 + 0.5 * t
        hidden[:, lo:hi] = (v * gate).astype(BF)
        slope = gate + 0.5 * v * (1.0 - t * t) * (0.7978845608 * (1.0 + 0.134145 * square))
        grad[:, lo:hi] = (mm_t(u, w2[lo:hi, :]) * slope).astype(BF)
    for lo, hi in cuts(w2.shape[1], 512):
        store(0, lo, hi, mm(hidden[...], w2[:, lo:hi]))
        store(1, lo, hi, mm_t(grad[...], w1[lo:hi, :]))


def near_kernel(rows, w1, w2, *rest):
    part, hidden, grad = rest[-3:]
    half = rows.shape[0] // 2

    def store(stream, lo, hi, value):
        part[stream * half : (stream + 1) * half, lo:hi] = value.astype(part.dtype)

    expert(rows[:half, :], rows[half:, :], w1, w2, hidden, grad, store)


def far_kernel(ours, theirs, w1, w2, keep, send, rows, hidden, grad):
    half = ours.shape[0] // 2
    for stream in range(2):
        at = slice(stream * half, (stream + 1) * half)
        rows[2 * stream * half : (2 * stream + 1) * half, :] = ours[at, :]
        rows[(2 * stream + 1) * half : (2 * stream + 2) * half, :] = theirs[at, :]

    def store(stream, lo, hi, value):
        at = slice(stream * half, (stream + 1) * half)
        keep[at, lo:hi] = value[:half, :]
        send[at, lo:hi] = value[half:, :].astype(send.dtype)

    expert(rows[: 2 * half, :], rows[2 * half :, :], w1, w2, hidden, grad, store)


def combine_kernel(keep, got, *outs):
    block = outs[0].shape[0] // 2
    for stream in range(2):
        for i, out in enumerate(outs):
            lo = (stream * len(outs) + i) * block
            at = slice(lo, lo + block)
            total = keep[at, :] + got[at, :].astype(F32)
            out[stream * block : (stream + 1) * block, :] = total.astype(out.dtype)


def add_kernel(a, b, after, out):
    out[...] = (a[...].astype(F32) + b[...].astype(F32)).astype(BF)


def final_kernel(mine, theirs, merge_high, merge_low, stream, gain, upstream, layer_out, stream_grad, back):
    rows, width = stream.shape
    n = mine.shape[0]
    rest = width - WIDE
    total = stream[...]
    centered, inverse = statistics(total)
    x_hat = centered * inverse
    for group in range(4):
        at = slice(group * rows, (group + 1) * rows)
        summed = mm(merge_high[at, :n], mine[...]) + mm(merge_high[at, n:], theirs[...])
        summed += mm(merge_low[at, :n], mine[...]) + mm(merge_low[at, n:], theirs[...])
        cols = slice(0, WIDE) if group < 2 else slice(WIDE, width)
        summed = summed if group < 2 else summed[:, :rest]
        if group % 2 == 0:
            layer_out[:, cols] = (total[:, cols] + summed).astype(BF)
        else:
            back[:, cols] = summed
    scaled = gain[...] * back[...]
    mean = jnp.mean(scaled, axis=-1, keepdims=True)
    along = jnp.mean(scaled * x_hat, axis=-1, keepdims=True)
    pulled = inverse * (scaled - mean - x_hat * along)
    stream_grad[...] = (upstream[...].astype(F32) + pulled).astype(BF)


def per_device(
    context,
    out_weight,
    residual,
    norm_gain,
    expert_in,
    expert_out,
    patch_index,
    patch_count,
    gate_value,
    upstream,
):
    rows, width = residual.shape
    experts, capacity = patch_index.shape
    shards = lax.axis_size("y")
    packed = experts * PACK
    block = experts * HALF
    units = expert_in.shape[2]
    sds = jax.ShapeDtypeStruct
    core = lax.axis_index("core")
    index = lax.axis_index("xz") * shards + lax.axis_index("y")
    ids = jnp.stack([core, index * (2 * rows)]).astype(I32)
    gain = norm_gain.reshape(1, width)

    def swap_core(x):
        return lax.ppermute(x, "core", [(0, 1), (1, 0)])

    def ring(x, way):
        pairs = []
        for y in range(shards):
            for c in range(2):
                step = way if c == 0 else -way
                pairs.append((y * 2 + c, (y + step) % shards * 2 + c))
        return lax.ppermute(x, ("y", "core"), pairs)

    def exchange(x):
        got = lax.all_to_all(
            x.reshape(experts, PACK, WIDE), "xz", split_axis=0, concat_axis=0, tiled=True
        )
        return got.reshape(packed, WIDE)

    weight_in = expert_in[0]
    weight_out = expert_out[0]

    with jax.named_scope("routing"):
        pick_keep, pick_send, slots = call(
            routing_kernel,
            [sds((packed, 4 * rows), BF)] * 2 + [sds((3 * experts, 128), BF)],
            [SMEM] + [VMEM] * 3,
            flops=10**9,
            moved=10**6,
        )(ids, patch_index, patch_count.reshape(1, experts), gate_value)
    with jax.named_scope("attend"):
        att_send, att_keep = call(
            attend_kernel,
            [sds((rows, width), F32)] * 2,
            [SMEM, VMEM, VMEM, ANY],
            flops=4 * rows * width * context.shape[1],
            moved=5 * 10**6,
        )(ids, context.T, out_weight, slots)
        att_got = swap_core(att_send)
    with jax.named_scope("norm"):
        stream, keep, send = call(
            norm_kernel,
            [sds((rows, width), F32)] + [sds((packed, WIDE), BF)] * 2,
            [VMEM] * 7,
            [pltpu.VMEM((2 * rows, width), BF)],
            flops=10**9,
            moved=3 * 10**6,
        )(att_keep, att_got, residual, gain, upstream, pick_keep, pick_send)
    with jax.named_scope("merge"):
        merge_high, merge_low = call(
            merge_kernel,
            [sds((4 * rows, 2 * packed), BF)] * 2,
            [SMEM, VMEM],
            flops=10**8,
            moved=10**6,
        )(ids, slots)
    pair = (2 * block, width)
    with jax.named_scope("dispatch"):
        own = call(unpack_kernel, sds(pair, BF), [VMEM], flops=10**8, moved=10**6)(
            exchange(keep + swap_core(send))
        )

    def near_part(x, kind, *after):
        tall = x.shape[0] // 2
        return call(
            near_kernel,
            sds(x.shape, kind),
            [VMEM] * 3 + [ANY] * len(after),
            [pltpu.VMEM((tall, units), BF)] * 2,
            flops=24 * tall * width * units,
            moved=10**7,
            mib=20,
        )(x, weight_in, weight_out, *after)

    def combine(keep, got, *kinds):
        outs = [sds(pair, kind) for kind in kinds]
        return call(combine_kernel, outs, [VMEM] * 2, flops=10**6, moved=10**6)(keep, got)

    with jax.named_scope("gather"):
        one = ring(own, 1)
        two = ring(own, -1)
        far = ring(one, 1)
        near = call(
            stack_kernel, sds((6 * block, width), BF), [VMEM] * 3, flops=10**5, moved=10**6
        )(own, one, two)
        near_send = swap_core(near)
        far_send = swap_core(far)
    with jax.named_scope("near"):
        near_keep = near_part(near, F32)
        near_got = swap_core(near_part(near_send, BF, near_keep, far))
        own_sum, one_sum, two_sum = combine(near_keep, near_got, F32, F32, BF)
        from_two = ring(two_sum, 1)
    with jax.named_scope("far"):
        far_keep, far_out = call(
            far_kernel,
            [sds(pair, F32), sds(pair, BF)],
            [VMEM] * 4,
            [pltpu.VMEM((4 * block, width), BF)] + [pltpu.VMEM((2 * block, units), BF)] * 2,
            flops=48 * block * width * units,
            moved=10**7,
            mib=20,
        )(far, far_send, weight_in, weight_out)
        (far_sum,) = combine(far_keep, swap_core(far_out), BF)
        from_far = ring(far_sum, -1)
    with jax.named_scope("reduce"):
        one_sum = call(
            add_kernel, sds(pair, BF), [VMEM] * 2 + [ANY], flops=10**5, moved=10**6
        )(one_sum, from_far, from_two)
        from_one = ring(one_sum, -1)
    with jax.named_scope("collect"):
        ready = call(
            pack_kernel,
            sds((packed, WIDE), BF),
            [VMEM] * 3,
            [pltpu.VMEM((packed, WIDE), BF)],
            flops=10**8,
            moved=10**6,
        )(own_sum, from_one, from_two)
        mine = exchange(ready)
        theirs = swap_core(mine)
    with jax.named_scope("final"):
        layer_out, stream_grad = call(
            final_kernel,
            [sds((rows, width), BF)] * 2,
            [VMEM] * 7,
            [pltpu.VMEM((rows, width), F32)],
            flops=10**9,
            moved=4 * 10**6,
        )(mine, theirs, merge_high, merge_low, stream, gain, upstream)
    return (layer_out, stream_grad)


def solution(mesh):
    sizes = mesh.devices.shape
    shards = 4
    split = Mesh(
        mesh.devices.reshape(sizes[0] // shards, shards, sizes[1]), ("xz", "y", "core")
    )
    return jax.shard_map(
        per_device,
        mesh=split,
        in_specs=(
            P(("xz", "y"), "core"),
            P("core", None),
            P(("xz", "y", "core"), None),
            P(),
            P(("xz", "y"), None, "core"),
            P(("xz", "y"), "core", None),
            P(),
            P(),
            P(),
            P(("xz", "y", "core"), None),
        ),
        out_specs=(P(("xz", "y", "core"), None), P(("xz", "y", "core"), None)),
        check_vma=False,
    )
```

```python
import jax
import jax.numpy as jnp
from jax import lax
from jax.experimental import pallas as pl
from jax.experimental.pallas import tpu as pltpu
from jax.sharding import Mesh, PartitionSpec as P

SLOTS = 4
HALF = 2
BF = jnp.bfloat16
F32 = jnp.float32
I32 = jnp.int32
VMEM = pl.BlockSpec(memory_space=pltpu.VMEM)
SMEM = pl.BlockSpec(memory_space=pltpu.SMEM)
ANY = pl.BlockSpec(memory_space=pl.ANY)
WIDE = 896
PACK = 8


def mm(a, b):
    return jnp.dot(a, b, preferred_element_type=F32)


def mm_t(a, b):
    return lax.dot_general(a, b, (((1,), (1,)), ((), ())), preferred_element_type=F32)


def mm_a(a, b):
    return lax.dot_general(a, b, (((0,), (0,)), ((), ())), preferred_element_type=F32)


def cuts(size, step):
    return [(i, min(i + step, size)) for i in range(0, size, step)]


def iota(shape, dim):
    return lax.broadcasted_iota(I32, shape, dim)


def call(kernel, outs, in_specs, scratch=(), flops=0, moved=0, mib=16):
    return pl.pallas_call(
        kernel,
        out_shape=outs,
        in_specs=in_specs,
        out_specs=jax.tree.map(lambda _: VMEM, outs),
        scratch_shapes=list(scratch),
        compiler_params=pltpu.CompilerParams(vmem_limit_bytes=mib * 2**20),
        cost_estimate=pl.CostEstimate(flops=flops, bytes_accessed=moved, transcendentals=0),
    )


def attend_kernel(ids, context, weight, send, keep):
    core = ids[0]
    rows = send.shape[0]
    for out, at in ((send, 1 - core), (keep, core)):
        block = context[:, pl.ds(pl.multiple_of(at * rows, rows), rows)]
        for lo, hi in cuts(out.shape[1], 512):
            out[:, lo:hi] = mm_a(block, weight[:, lo:hi])


def routing_kernel(ids, index, count, gate, pick_keep, pick_send, merge_high, merge_low):
    core = ids[0]
    experts, capacity = index.shape
    packed = experts * PACK
    own_rows = 128
    local = index[...] - ids[1]
    listed = iota((experts, capacity), 1) < count[...]
    mine = listed & (local >= 0) & (local < 2 * own_rows)
    upto = jnp.where(iota((capacity, capacity), 0) <= iota((capacity, capacity), 1), 1.0, 0.0)
    rank = mm(jnp.where(mine, 1.0, 0.0).astype(BF), upto.astype(BF))
    lane = iota((experts, 128), 1)
    rows = jnp.zeros((experts, 128), F32)
    gates = jnp.zeros((experts, 128), F32)
    shifted = (local + 1).astype(F32)
    for slot in range(SLOTS):
        here = mine & (rank == slot + 1.0)
        row = jnp.sum(jnp.where(here, shifted, 0.0), axis=1, keepdims=True) - 1.0
        rows = jnp.where(lane == slot, row, rows)
        weight = jnp.sum(jnp.where(here, gate[...], 0.0), axis=1, keepdims=True)
        gates = jnp.where(lane == slot, weight, gates)
    rows = rows.astype(BF)
    gate_high = gates.astype(BF)
    gate_low = (gates - gate_high.astype(F32)).astype(BF)
    spread = jnp.where(iota((packed, experts), 0) // PACK == iota((packed, experts), 1), 1.0, 0.0).astype(BF)
    down = mm(spread, rows)
    r_col = iota((packed, 128), 0) % PACK
    lane_id = iota((packed, 128), 1)
    k = iota((packed, 2 * own_rows), 1)
    r_wide = iota((packed, 2 * own_rows), 0) % PACK
    same_stream = (r_wide // 2) % 2 == k // own_rows
    patch = (core * own_rows + k % own_rows).astype(F32)
    for out, side in ((pick_keep, core), (pick_send, 1 - core)):
        slot = 2 * side + r_col % 2
        row = jnp.sum(jnp.where(lane_id == slot, down, 0.0), axis=1, keepdims=True)
        hot = same_stream & (row == patch)
        out[:, : 2 * own_rows] = jnp.where(hot & (r_wide < 4), 1.0, 0.0).astype(BF)
        out[:, 2 * own_rows :] = jnp.where(hot & (r_wide >= 4), 1.0, 0.0).astype(BF)
    along = (((0,), (1,)), ((), ()))
    across = [
        lax.dot_general(part, spread, along, preferred_element_type=F32)
        for part in (rows, gate_high, gate_low)
    ]
    q = iota((128, packed), 1) % PACK
    sub = iota((128, packed), 0)
    own = (core * own_rows + iota((own_rows, packed), 0)).astype(F32)
    for which, side in ((0, core), (1, 1 - core)):
        slot = 2 * side + q % 2
        row, high, low = (
            jnp.sum(jnp.where(sub == slot, part, 0.0), axis=0, keepdims=True) for part in across
        )
        hot = row == own
        for group in range(4):
            here = hot & (q // 2 == group)
            at = (slice(group * own_rows, (group + 1) * own_rows), slice(which * packed, (which + 1) * packed))
            merge_high[at] = jnp.where(here, high, 0.0).astype(BF)
            merge_low[at] = jnp.where(here, low, 0.0).astype(BF)


def statistics(stream):
    mean = jnp.mean(stream, axis=-1, keepdims=True)
    centered = stream - mean
    variance = jnp.mean(centered * centered, axis=-1, keepdims=True)
    return centered, lax.rsqrt(variance + 1e-06)


def norm_kernel(att_keep, att_got, residual, gain, upstream, pick_keep, pick_send, stream, keep, send, both):
    rows, width = residual.shape
    total = residual[...].astype(F32) + (att_keep[...] + att_got[...])
    stream[...] = total
    centered, inverse = statistics(total)
    both[:rows, :] = (gain[...] * centered * inverse).astype(BF)
    both[rows:, :] = upstream[...]
    rest = width - WIDE
    for pick, out in ((pick_send, send), (pick_keep, keep)):
        first, second = pick[:, : 2 * rows], pick[:, 2 * rows :]
        out[:, :rest] = (mm(first, both[:, :rest]) + mm(second, both[:, WIDE:])).astype(BF)
        out[:, rest:] = mm(first, both[:, rest:WIDE]).astype(BF)


def place(packed):
    q = packed
    return (q % 64 // 2) * PACK + q // 64 * 2 + q % 2


def unpack_kernel(got, first, second):
    n = got.shape[0]
    order = jnp.where(place(iota((n, n), 0)) == iota((n, n), 1), 1.0, 0.0).astype(BF)
    flat = mm(order, got[...]).astype(BF)
    quarter = n // 4
    rest = first.shape[1] - WIDE
    for stream, out in enumerate((first, second)):
        out[:, :WIDE] = flat[stream * quarter : (stream + 1) * quarter, :]
        out[:, WIDE:] = flat[(2 + stream) * quarter : (3 + stream) * quarter, :rest]


def pack_kernel(own_r, one_r, two_r, own_b, one_b, two_b, out, flat):
    n = out.shape[0]
    quarter = n // 4
    rest = own_r.shape[1] - WIDE
    flat[2 * quarter :, rest:] = jnp.zeros((2 * quarter, WIDE - rest), BF)
    for stream, (own, one, two) in enumerate(((own_r, one_r, two_r), (own_b, one_b, two_b))):
        total = (own[...] + one[...].astype(F32) + two[...].astype(F32)).astype(BF)
        flat[stream * quarter : (stream + 1) * quarter, :] = total[:, :WIDE]
        flat[(2 + stream) * quarter : (3 + stream) * quarter, :rest] = total[:, WIDE:]
    order = jnp.where(iota((n, n), 0) == place(iota((n, n), 1)), 1.0, 0.0).astype(BF)
    out[...] = mm(order, flat[...]).astype(BF)


def forward_kernel(x0, x1, x2, x3, w1, w2, *rest):
    slope, part, x, hidden = rest[-4:]
    block = x0.shape[0]
    for i, ref in enumerate((x0, x1, x2, x3)):
        x[i * block : (i + 1) * block, :] = ref[...]
    for lo, hi in cuts(hidden.shape[1], 256):
        v = mm(x[...], w1[:, lo:hi])
        square = v * v
        t = jnp.tanh(0.7978845608 * v * (1.0 + 0.044715 * square))
        gate = 0.5 + 0.5 * t
        hidden[:, lo:hi] = (v * gate).astype(BF)
        slope[:, lo:hi] = gate + 0.5 * v * (1.0 - t * t) * (0.7978845608 * (1.0 + 0.134145 * square))
    for lo, hi in cuts(part.shape[1], 512):
        part[:, lo:hi] = mm(hidden[...], w2[:, lo:hi]).astype(part.dtype)


def backward_kernel(x0, x1, x2, x3, w1, w2, slope, *rest):
    part, x, grad = rest[-3:]
    block = x0.shape[0]
    for i, ref in enumerate((x0, x1, x2, x3)):
        x[i * block : (i + 1) * block, :] = ref[...]
    for lo, hi in cuts(grad.shape[1], 256):
        grad[:, lo:hi] = (mm_t(x[...], w2[lo:hi, :]) * slope[:, lo:hi]).astype(BF)
    for lo, hi in cuts(part.shape[1], 512):
        part[:, lo:hi] = mm_t(grad[...], w1[lo:hi, :]).astype(part.dtype)


def combine_kernel(keep, got, own, one, two, far):
    block = own.shape[0]
    for i, out in enumerate((own, one, two, far)):
        at = slice(i * block, (i + 1) * block)
        out[...] = (keep[at, :] + got[at, :].astype(F32)).astype(out.dtype)


def add_kernel(a, b, out):
    out[...] = (a[...].astype(F32) + b[...].astype(F32)).astype(BF)


def final_kernel(mine, theirs, merge_high, merge_low, stream, gain, upstream, layer_out, stream_grad, back):
    rows, width = stream.shape
    n = mine.shape[0]
    rest = width - WIDE
    total = stream[...]
    centered, inverse = statistics(total)
    x_hat = centered * inverse
    for group in range(4):
        at = slice(group * rows, (group + 1) * rows)
        summed = mm(merge_high[at, :n], mine[...]) + mm(merge_high[at, n:], theirs[...])
        summed += mm(merge_low[at, :n], mine[...]) + mm(merge_low[at, n:], theirs[...])
        cols = slice(0, WIDE) if group < 2 else slice(WIDE, width)
        summed = summed if group < 2 else summed[:, :rest]
        if group % 2 == 0:
            layer_out[:, cols] = (total[:, cols] + summed).astype(BF)
        else:
            back[:, cols] = summed
    scaled = gain[...] * back[...]
    mean = jnp.mean(scaled, axis=-1, keepdims=True)
    along = jnp.mean(scaled * x_hat, axis=-1, keepdims=True)
    pulled = inverse * (scaled - mean - x_hat * along)
    stream_grad[...] = (upstream[...].astype(F32) + pulled).astype(BF)


def per_device(
    context,
    out_weight,
    residual,
    norm_gain,
    expert_in,
    expert_out,
    patch_index,
    patch_count,
    gate_value,
    upstream,
):
    rows, width = residual.shape
    experts, capacity = patch_index.shape
    shards = lax.axis_size("y")
    packed = experts * PACK
    block = experts * HALF
    units = expert_in.shape[2]
    sds = jax.ShapeDtypeStruct
    core = lax.axis_index("core")
    index = lax.axis_index("xz") * shards + lax.axis_index("y")
    ids = jnp.stack([core, index * (2 * rows)]).astype(I32)
    gain = norm_gain.reshape(1, width)

    def swap_core(x):
        return lax.ppermute(x, "core", [(0, 1), (1, 0)])

    def ring(x, way):
        pairs = []
        for y in range(shards):
            for c in range(2):
                step = way if c == 0 else -way
                pairs.append((y * 2 + c, (y + step) % shards * 2 + c))
        return lax.ppermute(x, ("y", "core"), pairs)

    def exchange(x):
        got = lax.all_to_all(
            x.reshape(experts, PACK, WIDE), "xz", split_axis=0, concat_axis=0, tiled=True
        )
        return got.reshape(packed, WIDE)

    with jax.named_scope("attend"):
        att_send, att_keep = call(
            attend_kernel,
            [sds((rows, width), F32)] * 2,
            [SMEM, VMEM, VMEM],
            flops=4 * rows * width * context.shape[1],
            moved=5 * 10**6,
        )(ids, context.T, out_weight)
        att_got = swap_core(att_send)
    with jax.named_scope("routing"):
        pick_keep, pick_send, merge_high, merge_low = call(
            routing_kernel,
            [sds((packed, 4 * rows), BF)] * 2 + [sds((4 * rows, 2 * packed), BF)] * 2,
            [SMEM] + [VMEM] * 3,
            flops=10**9,
            moved=2 * 10**6,
        )(ids, patch_index, patch_count.reshape(experts, 1), gate_value)
    with jax.named_scope("norm"):
        stream, keep, send = call(
            norm_kernel,
            [sds((rows, width), F32)] + [sds((packed, WIDE), BF)] * 2,
            [VMEM] * 7,
            [pltpu.VMEM((2 * rows, width), BF)],
            flops=10**9,
            moved=3 * 10**6,
        )(att_keep, att_got, residual, gain, upstream, pick_keep, pick_send)
    with jax.named_scope("dispatch"):
        got = exchange(keep + swap_core(send))
        normed_rows, down_rows = call(
            unpack_kernel, [sds((block, width), BF)] * 2, [VMEM], flops=10**8, moved=10**6
        )(got)

    def gather_y(own):
        one = ring(own, 1)
        two = ring(own, -1)
        far = ring(one, 1)
        keeps = [own, one, two, far]
        return keeps, [swap_core(x) for x in keeps]

    def combine(keep_part, send_part):
        return call(
            combine_kernel,
            [sds((block, width), F32)] * 2 + [sds((block, width), BF)] * 2,
            [VMEM] * 2,
            flops=10**6,
            moved=4 * 10**6,
        )(keep_part, swap_core(send_part))

    def reduce_y(parts):
        own, one, two, far = parts
        from_two = ring(two, 1)
        from_far = ring(far, -1)
        one = call(add_kernel, sds((block, width), BF), [VMEM] * 2, flops=10**5, moved=10**6)(one, from_far)
        return own, ring(one, -1), from_two

    weight_in = expert_in[0]
    weight_out = expert_out[0]
    tall = shards * block
    flops = 16 * tall * width * units

    def forward(xs, kind, *after):
        return call(
            forward_kernel,
            [sds((tall, units), F32), sds((tall, width), kind)],
            [VMEM] * 6 + [ANY] * len(after),
            [pltpu.VMEM((tall, width), BF), pltpu.VMEM((tall, units), BF)],
            flops=flops,
            moved=10**7,
            mib=24,
        )(*xs, weight_in, weight_out, *after)

    def backward(xs, slope, kind, *after):
        return call(
            backward_kernel,
            sds((tall, width), kind),
            [VMEM] * 7 + [ANY] * len(after),
            [pltpu.VMEM((tall, width), BF), pltpu.VMEM((tall, units), BF)],
            flops=flops,
            moved=10**7,
            mib=24,
        )(*xs, weight_in, weight_out, slope, *after)

    with jax.named_scope("gather_normed"):
        keeps, sends = gather_y(normed_rows)
    with jax.named_scope("gather_down"):
        down_keeps, down_sends = gather_y(down_rows)
    with jax.named_scope("forward"):
        slope_keep, part_keep = forward(keeps, F32)
        slope_send, part_send = forward(sends, BF, slope_keep)
    with jax.named_scope("return_result"):
        parts = combine(part_keep, part_send)
        result = reduce_y(parts)
    with jax.named_scope("backward"):
        back_send = backward(down_sends, slope_send, BF)
        back_keep = backward(down_keeps, slope_keep, F32, parts[3])
    with jax.named_scope("return_back"):
        back = reduce_y(combine(back_keep, back_send))
    with jax.named_scope("collect"):
        ready = call(
            pack_kernel,
            sds((packed, WIDE), BF),
            [VMEM] * 6,
            [pltpu.VMEM((packed, WIDE), BF)],
            flops=10**8,
            moved=10**6,
        )(*result, *back)
        mine = exchange(ready)
        theirs = swap_core(mine)
    with jax.named_scope("final"):
        layer_out, stream_grad = call(
            final_kernel,
            [sds((rows, width), BF)] * 2,
            [VMEM] * 7,
            [pltpu.VMEM((rows, width), F32)],
            flops=10**9,
            moved=4 * 10**6,
        )(mine, theirs, merge_high, merge_low, stream, gain, upstream)
    return (layer_out, stream_grad)


def solution(mesh):
    sizes = mesh.devices.shape
    shards = 4
    split = Mesh(
        mesh.devices.reshape(sizes[0] // shards, shards, sizes[1]), ("xz", "y", "core")
    )
    return jax.shard_map(
        per_device,
        mesh=split,
        in_specs=(
            P(("xz", "y"), "core"),
            P("core", None),
            P(("xz", "y", "core"), None),
            P(),
            P(("xz", "y"), None, "core"),
            P(("xz", "y"), "core", None),
            P(),
            P(),
            P(),
            P(("xz", "y", "core"), None),
        ),
        out_specs=(P(("xz", "y", "core"), None), P(("xz", "y", "core"), None)),
        check_vma=False,
    )
```

```python
import functools

import jax
import jax.numpy as jnp
from jax import lax
from jax.experimental import pallas as pl
from jax.experimental.pallas import tpu as pltpu
from jax.sharding import Mesh, PartitionSpec as P

SLOTS = 4
HALF = 2
BF = jnp.bfloat16
F32 = jnp.float32
I32 = jnp.int32
VMEM = pl.BlockSpec(memory_space=pltpu.VMEM)
SMEM = pl.BlockSpec(memory_space=pltpu.SMEM)
ANY = pl.BlockSpec(memory_space=pl.ANY)
WIDE = 896
PACK = 8


def mm(a, b):
    return jnp.dot(a, b, preferred_element_type=F32)


def mm_t(a, b):
    return lax.dot_general(a, b, (((1,), (1,)), ((), ())), preferred_element_type=F32)


def mm_a(a, b):
    return lax.dot_general(a, b, (((0,), (0,)), ((), ())), preferred_element_type=F32)


def cuts(size, step):
    return [(i, min(i + step, size)) for i in range(0, size, step)]


def iota(shape, dim):
    return lax.broadcasted_iota(I32, shape, dim)


def call(kernel, outs, in_specs, scratch=(), flops=0, moved=0, mib=16):
    return pl.pallas_call(
        kernel,
        out_shape=outs,
        in_specs=in_specs,
        out_specs=jax.tree.map(lambda _: VMEM, outs),
        scratch_shapes=list(scratch),
        compiler_params=pltpu.CompilerParams(vmem_limit_bytes=mib * 2**20),
        cost_estimate=pl.CostEstimate(flops=flops, bytes_accessed=moved, transcendentals=0),
    )


def attend_kernel(ids, context, weight, send, keep):
    core = ids[0]
    rows = send.shape[0]
    for out, at in ((send, 1 - core), (keep, core)):
        block = context[:, pl.ds(pl.multiple_of(at * rows, rows), rows)]
        for lo, hi in cuts(out.shape[1], 512):
            out[:, lo:hi] = mm_a(block, weight[:, lo:hi])


def routing_kernel(ids, index, count, gate, pick_keep, pick_send, merge_high, merge_low):
    core = ids[0]
    experts, capacity = index.shape
    packed = experts * PACK
    own_rows = 128
    local = index[...] - ids[1]
    listed = iota((experts, capacity), 1) < count[...]
    mine = listed & (local >= 0) & (local < 2 * own_rows)
    upto = jnp.where(iota((capacity, capacity), 0) <= iota((capacity, capacity), 1), 1.0, 0.0)
    rank = mm(jnp.where(mine, 1.0, 0.0).astype(BF), upto.astype(BF))
    lane = iota((experts, 128), 1)
    rows = jnp.zeros((experts, 128), F32)
    gates = jnp.zeros((experts, 128), F32)
    shifted = (local + 1).astype(F32)
    for slot in range(SLOTS):
        here = mine & (rank == slot + 1.0)
        row = jnp.sum(jnp.where(here, shifted, 0.0), axis=1, keepdims=True) - 1.0
        rows = jnp.where(lane == slot, row, rows)
        weight = jnp.sum(jnp.where(here, gate[...], 0.0), axis=1, keepdims=True)
        gates = jnp.where(lane == slot, weight, gates)
    rows = rows.astype(BF)
    gate_high = gates.astype(BF)
    gate_low = (gates - gate_high.astype(F32)).astype(BF)
    spread = jnp.where(iota((packed, experts), 0) // PACK == iota((packed, experts), 1), 1.0, 0.0).astype(BF)
    down = mm(spread, rows)
    r_col = iota((packed, 128), 0) % PACK
    lane_id = iota((packed, 128), 1)
    k = iota((packed, 2 * own_rows), 1)
    r_wide = iota((packed, 2 * own_rows), 0) % PACK
    same_stream = (r_wide // 2) % 2 == k // own_rows
    patch = (core * own_rows + k % own_rows).astype(F32)
    for out, side in ((pick_keep, core), (pick_send, 1 - core)):
        slot = 2 * side + r_col % 2
        row = jnp.sum(jnp.where(lane_id == slot, down, 0.0), axis=1, keepdims=True)
        hot = same_stream & (row == patch)
        out[:, : 2 * own_rows] = jnp.where(hot & (r_wide < 4), 1.0, 0.0).astype(BF)
        out[:, 2 * own_rows :] = jnp.where(hot & (r_wide >= 4), 1.0, 0.0).astype(BF)
    along = (((0,), (1,)), ((), ()))
    across = [
        lax.dot_general(part, spread, along, preferred_element_type=F32)
        for part in (rows, gate_high, gate_low)
    ]
    q = iota((128, packed), 1) % PACK
    sub = iota((128, packed), 0)
    own = (core * own_rows + iota((own_rows, packed), 0)).astype(F32)
    for which, side in ((0, core), (1, 1 - core)):
        slot = 2 * side + q % 2
        row, high, low = (
            jnp.sum(jnp.where(sub == slot, part, 0.0), axis=0, keepdims=True) for part in across
        )
        hot = row == own
        for group in range(4):
            here = hot & (q // 2 == group)
            at = (slice(group * own_rows, (group + 1) * own_rows), slice(which * packed, (which + 1) * packed))
            merge_high[at] = jnp.where(here, high, 0.0).astype(BF)
            merge_low[at] = jnp.where(here, low, 0.0).astype(BF)


def statistics(stream):
    mean = jnp.mean(stream, axis=-1, keepdims=True)
    centered = stream - mean
    variance = jnp.mean(centered * centered, axis=-1, keepdims=True)
    return centered, lax.rsqrt(variance + 1e-06)


def norm_kernel(att_keep, att_got, residual, gain, upstream, pick_keep, pick_send, stream, keep, send, both):
    rows, width = residual.shape
    total = residual[...].astype(F32) + (att_keep[...] + att_got[...])
    stream[...] = total
    centered, inverse = statistics(total)
    both[:rows, :] = (gain[...] * centered * inverse).astype(BF)
    both[rows:, :] = upstream[...]
    rest = width - WIDE
    for pick, out in ((pick_send, send), (pick_keep, keep)):
        first, second = pick[:, : 2 * rows], pick[:, 2 * rows :]
        out[:, :rest] = (mm(first, both[:, :rest]) + mm(second, both[:, WIDE:])).astype(BF)
        out[:, rest:] = mm(first, both[:, rest:WIDE]).astype(BF)


def place(packed):
    q = packed
    return (q % 64 // 2) * PACK + q // 64 * 2 + q % 2


def unpack_kernel(got, first, second):
    n = got.shape[0]
    order = jnp.where(place(iota((n, n), 0)) == iota((n, n), 1), 1.0, 0.0).astype(BF)
    flat = mm(order, got[...]).astype(BF)
    quarter = n // 4
    rest = first.shape[1] - WIDE
    for stream, out in enumerate((first, second)):
        out[:, :WIDE] = flat[stream * quarter : (stream + 1) * quarter, :]
        out[:, WIDE:] = flat[(2 + stream) * quarter : (3 + stream) * quarter, :rest]


def pack_kernel(own_r, one_r, two_r, own_b, one_b, two_b, out, flat):
    n = out.shape[0]
    quarter = n // 4
    rest = own_r.shape[1] - WIDE
    flat[2 * quarter :, rest:] = jnp.zeros((2 * quarter, WIDE - rest), BF)
    for stream, (own, one, two) in enumerate(((own_r, one_r, two_r), (own_b, one_b, two_b))):
        total = (own[...] + one[...].astype(F32) + two[...].astype(F32)).astype(BF)
        flat[stream * quarter : (stream + 1) * quarter, :] = total[:, :WIDE]
        flat[(2 + stream) * quarter : (3 + stream) * quarter, :rest] = total[:, WIDE:]
    order = jnp.where(iota((n, n), 0) == place(iota((n, n), 1)), 1.0, 0.0).astype(BF)
    out[...] = mm(order, flat[...]).astype(BF)


def gathered(refs, x):
    block = refs[0].shape[0]
    for i, ref in enumerate(refs):
        x[i * block : (i + 1) * block, :] = ref[...]


def scatter(value, parts, lo, hi):
    at = 0
    for part in parts:
        rows = part.shape[0]
        part[:, lo:hi] = value[at : at + rows, :].astype(part.dtype)
        at += rows


def forward_kernel(count, n_parts, *refs):
    w1, w2 = refs[count : count + 2]
    slope, *parts, x, hidden = refs[-3 - n_parts :]
    gathered(refs[:count], x)
    for lo, hi in cuts(hidden.shape[1], 256):
        v = mm(x[...], w1[:, lo:hi])
        square = v * v
        t = jnp.tanh(0.7978845608 * v * (1.0 + 0.044715 * square))
        gate = 0.5 + 0.5 * t
        hidden[:, lo:hi] = (v * gate).astype(BF)
        slope[:, lo:hi] = gate + 0.5 * v * (1.0 - t * t) * (0.7978845608 * (1.0 + 0.134145 * square))
    for lo, hi in cuts(w2.shape[1], 512):
        scatter(mm(hidden[...], w2[:, lo:hi]), parts, lo, hi)


def backward_kernel(count, n_parts, *refs):
    w1, w2, slope = refs[count : count + 3]
    *parts, x, grad = refs[-2 - n_parts :]
    gathered(refs[:count], x)
    for lo, hi in cuts(grad.shape[1], 256):
        grad[:, lo:hi] = (mm_t(x[...], w2[lo:hi, :]) * slope[:, lo:hi]).astype(BF)
    for lo, hi in cuts(w2.shape[1], 512):
        scatter(mm_t(grad[...], w1[lo:hi, :]), parts, lo, hi)


def combine_kernel(keep, got, *outs):
    block = outs[0].shape[0]
    for i, out in enumerate(outs):
        at = slice(i * block, (i + 1) * block)
        out[...] = (keep[at, :] + got[at, :].astype(F32)).astype(out.dtype)


def add_kernel(a, b, *rest):
    out = rest[-1]
    out[...] = (a[...].astype(F32) + b[...].astype(F32)).astype(BF)


def merged(rows, merge_high, merge_low, group, size, lo):
    at = (slice(group * size, (group + 1) * size), slice(lo, lo + rows.shape[0]))
    return mm(merge_high[at], rows[...]) + mm(merge_low[at], rows[...])


def first_kernel(mine, merge_high, merge_low, out):
    size = out.shape[0] // 4
    for group in range(4):
        at = slice(group * size, (group + 1) * size)
        out[at, :] = merged(mine, merge_high, merge_low, group, size, 0)


def final_kernel(first, theirs, merge_high, merge_low, stream, gain, upstream, layer_out, stream_grad, back):
    rows, width = stream.shape
    n = theirs.shape[0]
    rest = width - WIDE
    total = stream[...]
    centered, inverse = statistics(total)
    x_hat = centered * inverse
    for group in range(4):
        at = slice(group * rows, (group + 1) * rows)
        summed = first[at, :] + merged(theirs, merge_high, merge_low, group, rows, n)
        cols = slice(0, WIDE) if group < 2 else slice(WIDE, width)
        summed = summed if group < 2 else summed[:, :rest]
        if group % 2 == 0:
            layer_out[:, cols] = (total[:, cols] + summed).astype(BF)
        else:
            back[:, cols] = summed
    scaled = gain[...] * back[...]
    mean = jnp.mean(scaled, axis=-1, keepdims=True)
    along = jnp.mean(scaled * x_hat, axis=-1, keepdims=True)
    pulled = inverse * (scaled - mean - x_hat * along)
    stream_grad[...] = (upstream[...].astype(F32) + pulled).astype(BF)


def per_device(
    context,
    out_weight,
    residual,
    norm_gain,
    expert_in,
    expert_out,
    patch_index,
    patch_count,
    gate_value,
    upstream,
):
    rows, width = residual.shape
    experts, capacity = patch_index.shape
    shards = lax.axis_size("y")
    packed = experts * PACK
    block = experts * HALF
    units = expert_in.shape[2]
    sds = jax.ShapeDtypeStruct
    core = lax.axis_index("core")
    index = lax.axis_index("xz") * shards + lax.axis_index("y")
    ids = jnp.stack([core, index * (2 * rows)]).astype(I32)
    gain = norm_gain.reshape(1, width)

    def swap_core(x):
        return lax.ppermute(x, "core", [(0, 1), (1, 0)])

    def ring(x, way):
        pairs = []
        for y in range(shards):
            for c in range(2):
                step = way if c == 0 else -way
                pairs.append((y * 2 + c, (y + step) % shards * 2 + c))
        return lax.ppermute(x, ("y", "core"), pairs)

    def exchange(x):
        got = lax.all_to_all(
            x.reshape(experts, PACK, WIDE), "xz", split_axis=0, concat_axis=0, tiled=True
        )
        return got.reshape(packed, WIDE)

    with jax.named_scope("attend"):
        att_send, att_keep = call(
            attend_kernel,
            [sds((rows, width), F32)] * 2,
            [SMEM, VMEM, VMEM],
            flops=4 * rows * width * context.shape[1],
            moved=5 * 10**6,
        )(ids, context.T, out_weight)
        att_got = swap_core(att_send)
    with jax.named_scope("routing"):
        pick_keep, pick_send, merge_high, merge_low = call(
            routing_kernel,
            [sds((packed, 4 * rows), BF)] * 2 + [sds((4 * rows, 2 * packed), BF)] * 2,
            [SMEM] + [VMEM] * 3,
            flops=10**9,
            moved=2 * 10**6,
        )(ids, patch_index, patch_count.reshape(experts, 1), gate_value)
    with jax.named_scope("norm"):
        stream, keep, send = call(
            norm_kernel,
            [sds((rows, width), F32)] + [sds((packed, WIDE), BF)] * 2,
            [VMEM] * 7,
            [pltpu.VMEM((2 * rows, width), BF)],
            flops=10**9,
            moved=3 * 10**6,
        )(att_keep, att_got, residual, gain, upstream, pick_keep, pick_send)
    with jax.named_scope("dispatch"):
        got = exchange(keep + swap_core(send))
        normed_rows, down_rows = call(
            unpack_kernel, [sds((block, width), BF)] * 2, [VMEM], flops=10**8, moved=10**6
        )(got)

    weight_in = expert_in[0]
    weight_out = expert_out[0]
    single = (block, width)

    def gather_y(own):
        one = ring(own, 1)
        two = ring(own, -1)
        far = ring(one, 1)
        near = [own, one, two]
        return near, [swap_core(x) for x in near], [far, swap_core(far)]

    def combine(keep_part, got_part, *kinds):
        outs = [sds(single, kind) for kind in kinds]
        return call(combine_kernel, outs, [VMEM] * 2, flops=10**6, moved=10**6)(keep_part, got_part)

    def reduce_y(own, one, two, far, *after):
        from_two = ring(two, 1)
        from_far = ring(far, -1)
        specs = [VMEM] * 2 + [ANY] * (1 + len(after))
        one = call(add_kernel, sds(single, BF), specs, flops=10**5, moved=10**6)(
            one, from_far, from_two, *after
        )
        return own, ring(one, -1), from_two

    def expert(kernel, xs, weights, outs, after):
        tall = len(xs) * block
        parts = [sds((rows_of, width), kind) for rows_of, kind in outs]
        slope = [sds((tall, units), F32)] if kernel is forward_kernel else []
        return call(
            functools.partial(kernel, len(xs), len(parts)),
            slope + parts,
            [VMEM] * (len(xs) + len(weights)) + [ANY] * len(after),
            [pltpu.VMEM((tall, width), BF), pltpu.VMEM((tall, units), BF)],
            flops=16 * tall * width * units,
            moved=10**7,
            mib=24,
        )(*xs, *weights, *after)

    def forward(xs, outs, *after):
        return expert(forward_kernel, xs, (weight_in, weight_out), outs, after)

    def backward(xs, slope, outs, *after):
        return expert(backward_kernel, xs, (weight_in, weight_out, slope), outs, after)

    near_f32 = [(3 * block, F32)]
    near_bf = [(3 * block, BF)]
    far_both = [(block, F32), (block, BF)]
    with jax.named_scope("gather_normed"):
        near, near_send, far = gather_y(normed_rows)
    with jax.named_scope("gather_down"):
        down, down_send, down_far = gather_y(down_rows)
    with jax.named_scope("forward"):
        slope_keep, near_keep = forward(near, near_f32)
        slope_send, near_out = forward(near_send, near_bf, slope_keep)
        slope_far, far_keep, far_out = forward(far, far_both, slope_send)
        near_sums = combine(near_keep, swap_core(near_out), F32, F32, BF)
        far_sums = combine(far_keep, swap_core(far_out), BF)
    with jax.named_scope("backward"):
        (back_out,) = backward(down_send, slope_send, near_bf, slope_far)
        (back_keep,) = backward(down, slope_keep, near_f32, *far_sums)
        back_far, back_far_out = backward(down_far, slope_far, far_both)
        back_sums = combine(back_keep, swap_core(back_out), F32, F32, BF)
        back_far_sums = combine(back_far, swap_core(back_far_out), BF)
    with jax.named_scope("reduce"):
        result = reduce_y(*near_sums, *far_sums, back_sums[2])
        back = reduce_y(*back_sums, *back_far_sums)
    with jax.named_scope("collect"):
        ready = call(
            pack_kernel,
            sds((packed, WIDE), BF),
            [VMEM] * 6,
            [pltpu.VMEM((packed, WIDE), BF)],
            flops=10**8,
            moved=10**6,
        )(*result, *back)
        mine = exchange(ready)
        theirs = swap_core(mine)
    with jax.named_scope("final"):
        first = call(first_kernel, sds((4 * rows, WIDE), F32), [VMEM] * 3, flops=10**9, moved=4 * 10**6)(
            mine, merge_high, merge_low
        )
        layer_out, stream_grad = call(
            final_kernel,
            [sds((rows, width), BF)] * 2,
            [VMEM] * 7,
            [pltpu.VMEM((rows, width), F32)],
            flops=10**9,
            moved=4 * 10**6,
        )(first, theirs, merge_high, merge_low, stream, gain, upstream)
    return (layer_out, stream_grad)


def solution(mesh):
    sizes = mesh.devices.shape
    shards = 4
    split = Mesh(
        mesh.devices.reshape(sizes[0] // shards, shards, sizes[1]), ("xz", "y", "core")
    )
    return jax.shard_map(
        per_device,
        mesh=split,
        in_specs=(
            P(("xz", "y"), "core"),
            P("core", None),
            P(("xz", "y", "core"), None),
            P(),
            P(("xz", "y"), None, "core"),
            P(("xz", "y"), "core", None),
            P(),
            P(),
            P(),
            P(("xz", "y", "core"), None),
        ),
        out_specs=(P(("xz", "y", "core"), None), P(("xz", "y", "core"), None)),
        check_vma=False,
    )
```

```python
import jax
import jax.numpy as jnp
from jax import lax
from jax.experimental import pallas as pl
from jax.experimental.pallas import tpu as pltpu
from jax.sharding import Mesh, PartitionSpec as P

SLOTS = 4
HALF = 2
BF = jnp.bfloat16
F32 = jnp.float32
I32 = jnp.int32
VMEM = pl.BlockSpec(memory_space=pltpu.VMEM)
SMEM = pl.BlockSpec(memory_space=pltpu.SMEM)
ANY = pl.BlockSpec(memory_space=pl.ANY)
WIDE = 896
PACK = 8


def mm(a, b):
    return jnp.dot(a, b, preferred_element_type=F32)


def mm_t(a, b):
    return lax.dot_general(a, b, (((1,), (1,)), ((), ())), preferred_element_type=F32)


def mm_a(a, b):
    return lax.dot_general(a, b, (((0,), (0,)), ((), ())), preferred_element_type=F32)


def cuts(size, step):
    return [(i, min(i + step, size)) for i in range(0, size, step)]


def iota(shape, dim):
    return lax.broadcasted_iota(I32, shape, dim)


def call(kernel, outs, in_specs, scratch=(), flops=0, moved=0, mib=16):
    return pl.pallas_call(
        kernel,
        out_shape=outs,
        in_specs=in_specs,
        out_specs=jax.tree.map(lambda _: VMEM, outs),
        scratch_shapes=list(scratch),
        compiler_params=pltpu.CompilerParams(vmem_limit_bytes=mib * 2**20),
        cost_estimate=pl.CostEstimate(flops=flops, bytes_accessed=moved, transcendentals=0),
    )


def attend_kernel(ids, context, weight, send, keep):
    core = ids[0]
    rows = send.shape[0]
    for out, at in ((send, 1 - core), (keep, core)):
        block = context[:, pl.ds(pl.multiple_of(at * rows, rows), rows)]
        for lo, hi in cuts(out.shape[1], 512):
            out[:, lo:hi] = mm_a(block, weight[:, lo:hi])


def routing_kernel(ids, index, count, gate, pick_keep, pick_send, merge_high, merge_low):
    core = ids[0]
    experts, capacity = index.shape
    packed = experts * PACK
    own_rows = 128
    local = index[...] - ids[1]
    listed = iota((experts, capacity), 1) < count[...]
    mine = listed & (local >= 0) & (local < 2 * own_rows)
    upto = jnp.where(iota((capacity, capacity), 0) <= iota((capacity, capacity), 1), 1.0, 0.0)
    rank = mm(jnp.where(mine, 1.0, 0.0).astype(BF), upto.astype(BF))
    lane = iota((experts, 128), 1)
    rows = jnp.zeros((experts, 128), F32)
    gates = jnp.zeros((experts, 128), F32)
    shifted = (local + 1).astype(F32)
    for slot in range(SLOTS):
        here = mine & (rank == slot + 1.0)
        row = jnp.sum(jnp.where(here, shifted, 0.0), axis=1, keepdims=True) - 1.0
        rows = jnp.where(lane == slot, row, rows)
        weight = jnp.sum(jnp.where(here, gate[...], 0.0), axis=1, keepdims=True)
        gates = jnp.where(lane == slot, weight, gates)
    rows = rows.astype(BF)
    gate_high = gates.astype(BF)
    gate_low = (gates - gate_high.astype(F32)).astype(BF)
    spread = jnp.where(iota((packed, experts), 0) // PACK == iota((packed, experts), 1), 1.0, 0.0).astype(BF)
    down = mm(spread, rows)
    r_col = iota((packed, 128), 0) % PACK
    lane_id = iota((packed, 128), 1)
    k = iota((packed, 2 * own_rows), 1)
    r_wide = iota((packed, 2 * own_rows), 0) % PACK
    same_stream = (r_wide // 2) % 2 == k // own_rows
    patch = (core * own_rows + k % own_rows).astype(F32)
    for out, side in ((pick_keep, core), (pick_send, 1 - core)):
        slot = 2 * side + r_col % 2
        row = jnp.sum(jnp.where(lane_id == slot, down, 0.0), axis=1, keepdims=True)
        hot = same_stream & (row == patch)
        out[:, : 2 * own_rows] = jnp.where(hot & (r_wide < 4), 1.0, 0.0).astype(BF)
        out[:, 2 * own_rows :] = jnp.where(hot & (r_wide >= 4), 1.0, 0.0).astype(BF)
    along = (((0,), (1,)), ((), ()))
    across = [
        lax.dot_general(part, spread, along, preferred_element_type=F32)
        for part in (rows, gate_high, gate_low)
    ]
    q = iota((128, packed), 1) % PACK
    sub = iota((128, packed), 0)
    own = (core * own_rows + iota((own_rows, packed), 0)).astype(F32)
    for which, side in ((0, core), (1, 1 - core)):
        slot = 2 * side + q % 2
        row, high, low = (
            jnp.sum(jnp.where(sub == slot, part, 0.0), axis=0, keepdims=True) for part in across
        )
        hot = row == own
        for group in range(4):
            here = hot & (q // 2 == group)
            at = (slice(group * own_rows, (group + 1) * own_rows), slice(which * packed, (which + 1) * packed))
            merge_high[at] = jnp.where(here, high, 0.0).astype(BF)
            merge_low[at] = jnp.where(here, low, 0.0).astype(BF)


def statistics(stream):
    mean = jnp.mean(stream, axis=-1, keepdims=True)
    centered = stream - mean
    variance = jnp.mean(centered * centered, axis=-1, keepdims=True)
    return centered, lax.rsqrt(variance + 1e-06)


def norm_kernel(att_keep, att_got, residual, gain, upstream, pick_keep, pick_send, stream, keep, send, both):
    rows, width = residual.shape
    total = residual[...].astype(F32) + (att_keep[...] + att_got[...])
    stream[...] = total
    centered, inverse = statistics(total)
    both[:rows, :] = (gain[...] * centered * inverse).astype(BF)
    both[rows:, :] = upstream[...]
    rest = width - WIDE
    for pick, out in ((pick_send, send), (pick_keep, keep)):
        first, second = pick[:, : 2 * rows], pick[:, 2 * rows :]
        out[:, :rest] = (mm(first, both[:, :rest]) + mm(second, both[:, WIDE:])).astype(BF)
        out[:, rest:] = mm(first, both[:, rest:WIDE]).astype(BF)


def place(packed):
    q = packed
    return (q % 64 // 2) * PACK + q // 64 * 2 + q % 2


def unpack_kernel(got, first, second):
    n = got.shape[0]
    order = jnp.where(place(iota((n, n), 0)) == iota((n, n), 1), 1.0, 0.0).astype(BF)
    flat = mm(order, got[...]).astype(BF)
    quarter = n // 4
    rest = first.shape[1] - WIDE
    for stream, out in enumerate((first, second)):
        out[:, :WIDE] = flat[stream * quarter : (stream + 1) * quarter, :]
        out[:, WIDE:] = flat[(2 + stream) * quarter : (3 + stream) * quarter, :rest]


def pack_kernel(own_r, one_r, two_r, own_b, one_b, two_b, out, flat):
    n = out.shape[0]
    quarter = n // 4
    rest = own_r.shape[1] - WIDE
    flat[2 * quarter :, rest:] = jnp.zeros((2 * quarter, WIDE - rest), BF)
    for stream, (own, one, two) in enumerate(((own_r, one_r, two_r), (own_b, one_b, two_b))):
        total = (own[...] + one[...].astype(F32) + two[...].astype(F32)).astype(BF)
        flat[stream * quarter : (stream + 1) * quarter, :] = total[:, :WIDE]
        flat[(2 + stream) * quarter : (3 + stream) * quarter, :rest] = total[:, WIDE:]
    order = jnp.where(iota((n, n), 0) == place(iota((n, n), 1)), 1.0, 0.0).astype(BF)
    out[...] = mm(order, flat[...]).astype(BF)


def forward_kernel(x0, x1, x2, x3, w1, w2, *rest):
    slope, part, x, hidden = rest[-4:]
    block = x0.shape[0]
    for i, ref in enumerate((x0, x1, x2, x3)):
        x[i * block : (i + 1) * block, :] = ref[...]
    for lo, hi in cuts(hidden.shape[1], 256):
        v = mm(x[...], w1[:, lo:hi])
        square = v * v
        t = jnp.tanh(0.7978845608 * v * (1.0 + 0.044715 * square))
        gate = 0.5 + 0.5 * t
        hidden[:, lo:hi] = (v * gate).astype(BF)
        slope[:, lo:hi] = gate + 0.5 * v * (1.0 - t * t) * (0.7978845608 * (1.0 + 0.134145 * square))
    for lo, hi in cuts(part.shape[1], 512):
        part[:, lo:hi] = mm(hidden[...], w2[:, lo:hi]).astype(part.dtype)


def backward_kernel(x0, x1, x2, x3, w1, w2, slope, *rest):
    part, x, grad = rest[-3:]
    block = x0.shape[0]
    for i, ref in enumerate((x0, x1, x2, x3)):
        x[i * block : (i + 1) * block, :] = ref[...]
    for lo, hi in cuts(grad.shape[1], 256):
        grad[:, lo:hi] = (mm_t(x[...], w2[lo:hi, :]) * slope[:, lo:hi]).astype(BF)
    for lo, hi in cuts(part.shape[1], 512):
        part[:, lo:hi] = mm_t(grad[...], w1[lo:hi, :]).astype(part.dtype)


def combine_kernel(keep, got, own, one, two, far):
    block = own.shape[0]
    for i, out in enumerate((own, one, two, far)):
        at = slice(i * block, (i + 1) * block)
        out[...] = (keep[at, :] + got[at, :].astype(F32)).astype(out.dtype)


def add_kernel(a, b, *rest):
    out = rest[-1]
    out[...] = (a[...].astype(F32) + b[...].astype(F32)).astype(BF)


def merged(rows, merge_high, merge_low, group, size, lo):
    at = (slice(group * size, (group + 1) * size), slice(lo, lo + rows.shape[0]))
    return mm(merge_high[at], rows[...]) + mm(merge_low[at], rows[...])


def first_kernel(mine, merge_high, merge_low, out):
    size = out.shape[0] // 4
    for group in range(4):
        at = slice(group * size, (group + 1) * size)
        out[at, :] = merged(mine, merge_high, merge_low, group, size, 0)


def final_kernel(first, theirs, merge_high, merge_low, stream, gain, upstream, layer_out, stream_grad, back):
    rows, width = stream.shape
    n = theirs.shape[0]
    rest = width - WIDE
    total = stream[...]
    centered, inverse = statistics(total)
    x_hat = centered * inverse
    for group in range(4):
        at = slice(group * rows, (group + 1) * rows)
        summed = first[at, :] + merged(theirs, merge_high, merge_low, group, rows, n)
        cols = slice(0, WIDE) if group < 2 else slice(WIDE, width)
        summed = summed if group < 2 else summed[:, :rest]
        if group % 2 == 0:
            layer_out[:, cols] = (total[:, cols] + summed).astype(BF)
        else:
            back[:, cols] = summed
    scaled = gain[...] * back[...]
    mean = jnp.mean(scaled, axis=-1, keepdims=True)
    along = jnp.mean(scaled * x_hat, axis=-1, keepdims=True)
    pulled = inverse * (scaled - mean - x_hat * along)
    stream_grad[...] = (upstream[...].astype(F32) + pulled).astype(BF)


def per_device(
    context,
    out_weight,
    residual,
    norm_gain,
    expert_in,
    expert_out,
    patch_index,
    patch_count,
    gate_value,
    upstream,
):
    rows, width = residual.shape
    experts, capacity = patch_index.shape
    shards = lax.axis_size("y")
    packed = experts * PACK
    block = experts * HALF
    units = expert_in.shape[2]
    sds = jax.ShapeDtypeStruct
    core = lax.axis_index("core")
    index = lax.axis_index("xz") * shards + lax.axis_index("y")
    ids = jnp.stack([core, index * (2 * rows)]).astype(I32)
    gain = norm_gain.reshape(1, width)

    def swap_core(x):
        return lax.ppermute(x, "core", [(0, 1), (1, 0)])

    def ring(x, way):
        pairs = []
        for y in range(shards):
            for c in range(2):
                step = way if c == 0 else -way
                pairs.append((y * 2 + c, (y + step) % shards * 2 + c))
        return lax.ppermute(x, ("y", "core"), pairs)

    def exchange(x):
        got = lax.all_to_all(
            x.reshape(experts, PACK, WIDE), "xz", split_axis=0, concat_axis=0, tiled=True
        )
        return got.reshape(packed, WIDE)

    with jax.named_scope("attend"):
        att_send, att_keep = call(
            attend_kernel,
            [sds((rows, width), F32)] * 2,
            [SMEM, VMEM, VMEM],
            flops=4 * rows * width * context.shape[1],
            moved=5 * 10**6,
        )(ids, context.T, out_weight)
        att_got = swap_core(att_send)
    with jax.named_scope("routing"):
        pick_keep, pick_send, merge_high, merge_low = call(
            routing_kernel,
            [sds((packed, 4 * rows), BF)] * 2 + [sds((4 * rows, 2 * packed), BF)] * 2,
            [SMEM] + [VMEM] * 3,
            flops=10**9,
            moved=2 * 10**6,
        )(ids, patch_index, patch_count.reshape(experts, 1), gate_value)
    with jax.named_scope("norm"):
        stream, keep, send = call(
            norm_kernel,
            [sds((rows, width), F32)] + [sds((packed, WIDE), BF)] * 2,
            [VMEM] * 7,
            [pltpu.VMEM((2 * rows, width), BF)],
            flops=10**9,
            moved=3 * 10**6,
        )(att_keep, att_got, residual, gain, upstream, pick_keep, pick_send)
    with jax.named_scope("dispatch"):
        got = exchange(keep + swap_core(send))
        normed_rows, down_rows = call(
            unpack_kernel, [sds((block, width), BF)] * 2, [VMEM], flops=10**8, moved=10**6
        )(got)

    def gather_y(own):
        one = ring(own, 1)
        two = ring(own, -1)
        far = ring(one, 1)
        keeps = [own, one, two, far]
        return keeps, [swap_core(x) for x in keeps]

    def combine(keep_part, send_part):
        return call(
            combine_kernel,
            [sds((block, width), F32)] * 2 + [sds((block, width), BF)] * 2,
            [VMEM] * 2,
            flops=10**6,
            moved=4 * 10**6,
        )(keep_part, swap_core(send_part))

    def reduce_y(parts, early):
        own, one, two, far = parts
        from_far = ring(far, -1)
        from_two = ring(two, 1)
        after = [from_two] if early else []
        one = call(
            add_kernel, sds((block, width), BF), [VMEM] * 2 + [ANY] * len(after), flops=10**5, moved=10**6
        )(one, from_far, *after)
        return own, ring(one, -1), from_two

    weight_in = expert_in[0]
    weight_out = expert_out[0]
    tall = shards * block
    flops = 16 * tall * width * units

    def forward(xs, kind, *after):
        return call(
            forward_kernel,
            [sds((tall, units), F32), sds((tall, width), kind)],
            [VMEM] * 6 + [ANY] * len(after),
            [pltpu.VMEM((tall, width), BF), pltpu.VMEM((tall, units), BF)],
            flops=flops,
            moved=10**7,
            mib=24,
        )(*xs, weight_in, weight_out, *after)

    def backward(xs, slope, kind, *after):
        return call(
            backward_kernel,
            sds((tall, width), kind),
            [VMEM] * 7 + [ANY] * len(after),
            [pltpu.VMEM((tall, width), BF), pltpu.VMEM((tall, units), BF)],
            flops=flops,
            moved=10**7,
            mib=24,
        )(*xs, weight_in, weight_out, slope, *after)

    with jax.named_scope("gather_normed"):
        keeps, sends = gather_y(normed_rows)
    with jax.named_scope("gather_down"):
        down_keeps, down_sends = gather_y(down_rows)
    with jax.named_scope("forward"):
        slope_keep, part_keep = forward(keeps, F32)
        slope_send, part_send = forward(sends, BF, slope_keep)
    with jax.named_scope("return_result"):
        parts = combine(part_keep, part_send)
        result = reduce_y(parts, True)
    with jax.named_scope("backward"):
        back_send = backward(down_sends, slope_send, BF)
        back_keep = backward(down_keeps, slope_keep, F32, parts[3])
    with jax.named_scope("return_back"):
        back = reduce_y(combine(back_keep, back_send), False)
    with jax.named_scope("collect"):
        ready = call(
            pack_kernel,
            sds((packed, WIDE), BF),
            [VMEM] * 6,
            [pltpu.VMEM((packed, WIDE), BF)],
            flops=10**8,
            moved=10**6,
        )(*result, *back)
        mine = exchange(ready)
        theirs = swap_core(mine)
    with jax.named_scope("final"):
        first = call(first_kernel, sds((4 * rows, WIDE), F32), [VMEM] * 3, flops=10**9, moved=4 * 10**6)(
            mine, merge_high, merge_low
        )
        layer_out, stream_grad = call(
            final_kernel,
            [sds((rows, width), BF)] * 2,
            [VMEM] * 7,
            [pltpu.VMEM((rows, width), F32)],
            flops=10**9,
            moved=4 * 10**6,
        )(first, theirs, merge_high, merge_low, stream, gain, upstream)
    return (layer_out, stream_grad)


def solution(mesh):
    sizes = mesh.devices.shape
    shards = 4
    split = Mesh(
        mesh.devices.reshape(sizes[0] // shards, shards, sizes[1]), ("xz", "y", "core")
    )
    return jax.shard_map(
        per_device,
        mesh=split,
        in_specs=(
            P(("xz", "y"), "core"),
            P("core", None),
            P(("xz", "y", "core"), None),
            P(),
            P(("xz", "y"), None, "core"),
            P(("xz", "y"), "core", None),
            P(),
            P(),
            P(),
            P(("xz", "y", "core"), None),
        ),
        out_specs=(P(("xz", "y", "core"), None), P(("xz", "y", "core"), None)),
        check_vma=False,
    )
```

```python
import functools

import jax
import jax.numpy as jnp
from jax import lax
from jax.experimental import pallas as pl
from jax.experimental.pallas import tpu as pltpu
from jax.sharding import Mesh, PartitionSpec as P

SLOTS = 4
HALF = 2
BF = jnp.bfloat16
F32 = jnp.float32
I32 = jnp.int32
VMEM = pl.BlockSpec(memory_space=pltpu.VMEM)
SMEM = pl.BlockSpec(memory_space=pltpu.SMEM)
ANY = pl.BlockSpec(memory_space=pl.ANY)
WIDE = 896
PACK = 8


def mm(a, b):
    return jnp.dot(a, b, preferred_element_type=F32)


def mm_t(a, b):
    return lax.dot_general(a, b, (((1,), (1,)), ((), ())), preferred_element_type=F32)


def mm_a(a, b):
    return lax.dot_general(a, b, (((0,), (0,)), ((), ())), preferred_element_type=F32)


def cuts(size, step):
    return [(i, min(i + step, size)) for i in range(0, size, step)]


def iota(shape, dim):
    return lax.broadcasted_iota(I32, shape, dim)


def call(kernel, outs, in_specs, scratch=(), flops=0, moved=0, mib=16):
    return pl.pallas_call(
        kernel,
        out_shape=outs,
        in_specs=in_specs,
        out_specs=jax.tree.map(lambda _: VMEM, outs),
        scratch_shapes=list(scratch),
        compiler_params=pltpu.CompilerParams(vmem_limit_bytes=mib * 2**20),
        cost_estimate=pl.CostEstimate(flops=flops, bytes_accessed=moved, transcendentals=0),
    )


def attend_kernel(other, ids, context, weight, out):
    at = (1 - ids[0]) if other else ids[0]
    rows = out.shape[0]
    block = context[:, pl.ds(pl.multiple_of(at * rows, rows), rows)]
    for lo, hi in cuts(out.shape[1], 512):
        out[:, lo:hi] = mm_a(block, weight[:, lo:hi])


def routing_kernel(ids, index, count, gate, pick_keep, pick_send, slots):
    core = ids[0]
    experts, capacity = index.shape
    packed = experts * PACK
    rows = pick_keep.shape[1] // 4
    local = index[...] - ids[1]
    diagonal = iota((experts, experts), 0) == iota((experts, experts), 1)
    counts = jnp.sum(jnp.where(diagonal, count[...].astype(F32), 0.0), axis=1, keepdims=True)
    listed = iota((experts, capacity), 1).astype(F32) < counts
    mine = listed & (local >= 0) & (local < 2 * rows)
    upto = jnp.where(iota((capacity, capacity), 0) <= iota((capacity, capacity), 1), 1.0, 0.0)
    rank = mm(jnp.where(mine, 1.0, 0.0).astype(BF), upto.astype(BF))
    lane = iota((experts, 128), 1)
    at_row = jnp.zeros((experts, 128), F32)
    gates = jnp.zeros((experts, 128), F32)
    shifted = (local + 1).astype(F32)
    for slot in range(SLOTS):
        here = mine & (rank == slot + 1.0)
        row = jnp.sum(jnp.where(here, shifted, 0.0), axis=1, keepdims=True) - 1.0
        at_row = jnp.where(lane == slot, row, at_row)
        value = jnp.sum(jnp.where(here, gate[...], 0.0), axis=1, keepdims=True)
        gates = jnp.where(lane == slot, value, gates)
    at_row = at_row.astype(BF)
    gate_high = gates.astype(BF)
    slots[:experts, :] = at_row
    slots[experts : 2 * experts, :] = gate_high
    slots[2 * experts :, :] = (gates - gate_high.astype(F32)).astype(BF)
    down = mm(spread_of(experts), at_row)
    r_col = iota((packed, 128), 0) % PACK
    lane_id = iota((packed, 128), 1)
    k = iota((packed, 2 * rows), 1)
    r_wide = iota((packed, 2 * rows), 0) % PACK
    same_stream = (r_wide // 2) % 2 == k // rows
    patch = (core * rows + k % rows).astype(F32)
    for out, side in ((pick_keep, core), (pick_send, 1 - core)):
        slot = 2 * side + r_col % 2
        row = jnp.sum(jnp.where(lane_id == slot, down, 0.0), axis=1, keepdims=True)
        hot = same_stream & (row == patch)
        out[:, : 2 * rows] = jnp.where(hot & (r_wide < 4), 1.0, 0.0).astype(BF)
        out[:, 2 * rows :] = jnp.where(hot & (r_wide >= 4), 1.0, 0.0).astype(BF)


def spread_of(experts):
    shape = (experts * PACK, experts)
    return jnp.where(iota(shape, 0) // PACK == iota(shape, 1), 1.0, 0.0).astype(BF)


def merge_kernel(ids, slots, merge_high, merge_low):
    core = ids[0]
    experts = slots.shape[0] // 3
    packed = experts * PACK
    rows = merge_high.shape[0] // 4
    spread = spread_of(experts)
    across = [
        lax.dot_general(
            slots[i * experts : (i + 1) * experts, :],
            spread,
            (((0,), (1,)), ((), ())),
            preferred_element_type=F32,
        )
        for i in range(3)
    ]
    q = iota((128, packed), 1) % PACK
    sub = iota((128, packed), 0)
    own = (core * rows + iota((rows, packed), 0)).astype(F32)
    q_rows = iota((rows, packed), 1) % PACK
    for which, side in ((0, core), (1, 1 - core)):
        slot = 2 * side + q % 2
        row, high, low = (
            jnp.sum(jnp.where(sub == slot, part, 0.0), axis=0, keepdims=True) for part in across
        )
        hot = row == own
        for group in range(4):
            here = hot & (q_rows // 2 == group)
            at = (slice(group * rows, (group + 1) * rows), slice(which * packed, (which + 1) * packed))
            merge_high[at] = jnp.where(here, high, 0.0).astype(BF)
            merge_low[at] = jnp.where(here, low, 0.0).astype(BF)


def statistics(stream):
    mean = jnp.mean(stream, axis=-1, keepdims=True)
    centered = stream - mean
    variance = jnp.mean(centered * centered, axis=-1, keepdims=True)
    return centered, lax.rsqrt(variance + 1e-06)


def norm_kernel(att_keep, att_got, residual, gain, upstream, pick_keep, pick_send, stream, keep, send, both):
    rows, width = residual.shape
    total = residual[...].astype(F32) + (att_keep[...] + att_got[...])
    stream[...] = total
    centered, inverse = statistics(total)
    both[:rows, :] = (gain[...] * centered * inverse).astype(BF)
    both[rows:, :] = upstream[...]
    rest = width - WIDE
    for pick, out in ((pick_send, send), (pick_keep, keep)):
        first, second = pick[:, : 2 * rows], pick[:, 2 * rows :]
        out[:, :rest] = (mm(first, both[:, :rest]) + mm(second, both[:, WIDE:])).astype(BF)
        out[:, rest:] = mm(first, both[:, rest:WIDE]).astype(BF)


def place(packed):
    q = packed
    return (q % 64 // 2) * PACK + q // 64 * 2 + q % 2


def unpack_kernel(got, first, second):
    n = got.shape[0]
    order = jnp.where(place(iota((n, n), 0)) == iota((n, n), 1), 1.0, 0.0).astype(BF)
    flat = mm(order, got[...]).astype(BF)
    quarter = n // 4
    rest = first.shape[1] - WIDE
    for stream, out in enumerate((first, second)):
        out[:, :WIDE] = flat[stream * quarter : (stream + 1) * quarter, :]
        out[:, WIDE:] = flat[(2 + stream) * quarter : (3 + stream) * quarter, :rest]


def pack_kernel(own_r, one_r, two_r, own_b, one_b, two_b, out, flat):
    n = out.shape[0]
    quarter = n // 4
    rest = own_r.shape[1] - WIDE
    flat[2 * quarter :, rest:] = jnp.zeros((2 * quarter, WIDE - rest), BF)
    for stream, (own, one, two) in enumerate(((own_r, one_r, two_r), (own_b, one_b, two_b))):
        total = (own[...] + one[...].astype(F32) + two[...].astype(F32)).astype(BF)
        flat[stream * quarter : (stream + 1) * quarter, :] = total[:, :WIDE]
        flat[(2 + stream) * quarter : (3 + stream) * quarter, :rest] = total[:, WIDE:]
    order = jnp.where(iota((n, n), 0) == place(iota((n, n), 1)), 1.0, 0.0).astype(BF)
    out[...] = mm(order, flat[...]).astype(BF)


def forward_kernel(x0, x1, x2, x3, w1, w2, *rest):
    slope, part, x, hidden = rest[-4:]
    block = x0.shape[0]
    for i, ref in enumerate((x0, x1, x2, x3)):
        x[i * block : (i + 1) * block, :] = ref[...]
    for lo, hi in cuts(hidden.shape[1], 256):
        v = mm(x[...], w1[:, lo:hi])
        square = v * v
        t = jnp.tanh(0.7978845608 * v * (1.0 + 0.044715 * square))
        gate = 0.5 + 0.5 * t
        hidden[:, lo:hi] = (v * gate).astype(BF)
        slope[:, lo:hi] = gate + 0.5 * v * (1.0 - t * t) * (0.7978845608 * (1.0 + 0.134145 * square))
    for lo, hi in cuts(part.shape[1], 512):
        part[:, lo:hi] = mm(hidden[...], w2[:, lo:hi]).astype(part.dtype)


def backward_kernel(x0, x1, x2, x3, w1, w2, slope, *rest):
    part, x, grad = rest[-3:]
    block = x0.shape[0]
    for i, ref in enumerate((x0, x1, x2, x3)):
        x[i * block : (i + 1) * block, :] = ref[...]
    for lo, hi in cuts(grad.shape[1], 256):
        grad[:, lo:hi] = (mm_t(x[...], w2[lo:hi, :]) * slope[:, lo:hi]).astype(BF)
    for lo, hi in cuts(part.shape[1], 512):
        part[:, lo:hi] = mm_t(grad[...], w1[lo:hi, :]).astype(part.dtype)


def combine_kernel(keep, got, own, one, two, far):
    block = own.shape[0]
    for i, out in enumerate((own, one, two, far)):
        at = slice(i * block, (i + 1) * block)
        out[...] = (keep[at, :] + got[at, :].astype(F32)).astype(out.dtype)


def add_kernel(a, b, out):
    out[...] = (a[...].astype(F32) + b[...].astype(F32)).astype(BF)


def merged(rows, merge_high, merge_low, group, size, lo):
    at = (slice(group * size, (group + 1) * size), slice(lo, lo + rows.shape[0]))
    return mm(merge_high[at], rows[...]) + mm(merge_low[at], rows[...])


def first_kernel(mine, merge_high, merge_low, out):
    size = out.shape[0] // 4
    for group in range(4):
        at = slice(group * size, (group + 1) * size)
        out[at, :] = merged(mine, merge_high, merge_low, group, size, 0)


def final_kernel(first, theirs, merge_high, merge_low, stream, gain, upstream, layer_out, stream_grad, back):
    rows, width = stream.shape
    n = theirs.shape[0]
    rest = width - WIDE
    total = stream[...]
    centered, inverse = statistics(total)
    x_hat = centered * inverse
    for group in range(4):
        at = slice(group * rows, (group + 1) * rows)
        summed = first[at, :] + merged(theirs, merge_high, merge_low, group, rows, n)
        cols = slice(0, WIDE) if group < 2 else slice(WIDE, width)
        summed = summed if group < 2 else summed[:, :rest]
        if group % 2 == 0:
            layer_out[:, cols] = (total[:, cols] + summed).astype(BF)
        else:
            back[:, cols] = summed
    scaled = gain[...] * back[...]
    mean = jnp.mean(scaled, axis=-1, keepdims=True)
    along = jnp.mean(scaled * x_hat, axis=-1, keepdims=True)
    pulled = inverse * (scaled - mean - x_hat * along)
    stream_grad[...] = (upstream[...].astype(F32) + pulled).astype(BF)


def per_device(
    context,
    out_weight,
    residual,
    norm_gain,
    expert_in,
    expert_out,
    patch_index,
    patch_count,
    gate_value,
    upstream,
):
    rows, width = residual.shape
    experts, capacity = patch_index.shape
    shards = lax.axis_size("y")
    packed = experts * PACK
    block = experts * HALF
    units = expert_in.shape[2]
    sds = jax.ShapeDtypeStruct
    core = lax.axis_index("core")
    index = lax.axis_index("xz") * shards + lax.axis_index("y")
    ids = jnp.stack([core, index * (2 * rows)]).astype(I32)
    gain = norm_gain.reshape(1, width)

    def swap_core(x):
        return lax.ppermute(x, "core", [(0, 1), (1, 0)])

    def ring(x, way):
        pairs = []
        for y in range(shards):
            for c in range(2):
                step = way if c == 0 else -way
                pairs.append((y * 2 + c, (y + step) % shards * 2 + c))
        return lax.ppermute(x, ("y", "core"), pairs)

    def exchange(x):
        got = lax.all_to_all(
            x.reshape(experts, PACK, WIDE), "xz", split_axis=0, concat_axis=0, tiled=True
        )
        return got.reshape(packed, WIDE)

    def attend(other):
        return call(
            functools.partial(attend_kernel, other),
            sds((rows, width), F32),
            [SMEM, VMEM, VMEM],
            flops=2 * rows * width * context.shape[1],
            moved=4 * 10**6,
        )(ids, context.T, out_weight)

    with jax.named_scope("attend"):
        att_got = swap_core(attend(True))
        att_keep = attend(False)
    with jax.named_scope("routing"):
        pick_keep, pick_send, slots = call(
            routing_kernel,
            [sds((packed, 4 * rows), BF)] * 2 + [sds((3 * experts, 128), BF)],
            [SMEM] + [VMEM] * 3,
            flops=10**9,
            moved=10**6,
        )(ids, patch_index, patch_count.reshape(1, experts), gate_value)
    with jax.named_scope("merge"):
        merge_high, merge_low = call(
            merge_kernel,
            [sds((4 * rows, 2 * packed), BF)] * 2,
            [SMEM, VMEM],
            flops=10**8,
            moved=10**6,
        )(ids, slots)
    with jax.named_scope("norm"):
        stream, keep, send = call(
            norm_kernel,
            [sds((rows, width), F32)] + [sds((packed, WIDE), BF)] * 2,
            [VMEM] * 7,
            [pltpu.VMEM((2 * rows, width), BF)],
            flops=10**9,
            moved=3 * 10**6,
        )(att_keep, att_got, residual, gain, upstream, pick_keep, pick_send)
    with jax.named_scope("dispatch"):
        got = exchange(keep + swap_core(send))
        normed_rows, down_rows = call(
            unpack_kernel, [sds((block, width), BF)] * 2, [VMEM], flops=10**8, moved=10**6
        )(got)

    def gather_y(own):
        one = ring(own, 1)
        two = ring(own, -1)
        far = ring(one, 1)
        keeps = [own, one, two, far]
        return keeps, [swap_core(x) for x in keeps]

    def combine(keep_part, send_part):
        return call(
            combine_kernel,
            [sds((block, width), F32)] * 2 + [sds((block, width), BF)] * 2,
            [VMEM] * 2,
            flops=10**6,
            moved=4 * 10**6,
        )(keep_part, swap_core(send_part))

    def reduce_y(parts):
        own, one, two, far = parts
        from_two = ring(two, 1)
        from_far = ring(far, -1)
        one = call(add_kernel, sds((block, width), BF), [VMEM] * 2, flops=10**5, moved=10**6)(one, from_far)
        return own, ring(one, -1), from_two

    weight_in = expert_in[0]
    weight_out = expert_out[0]
    tall = shards * block
    flops = 16 * tall * width * units

    def forward(xs, kind, *after):
        return call(
            forward_kernel,
            [sds((tall, units), F32), sds((tall, width), kind)],
            [VMEM] * 6 + [ANY] * len(after),
            [pltpu.VMEM((tall, width), BF), pltpu.VMEM((tall, units), BF)],
            flops=flops,
            moved=10**7,
            mib=24,
        )(*xs, weight_in, weight_out, *after)

    def backward(xs, slope, kind, *after):
        return call(
            backward_kernel,
            sds((tall, width), kind),
            [VMEM] * 7 + [ANY] * len(after),
            [pltpu.VMEM((tall, width), BF), pltpu.VMEM((tall, units), BF)],
            flops=flops,
            moved=10**7,
            mib=24,
        )(*xs, weight_in, weight_out, slope, *after)

    with jax.named_scope("gather_normed"):
        keeps, sends = gather_y(normed_rows)
    with jax.named_scope("gather_down"):
        down_keeps, down_sends = gather_y(down_rows)
    with jax.named_scope("forward"):
        slope_keep, part_keep = forward(keeps, F32)
        slope_send, part_send = forward(sends, BF, slope_keep)
    with jax.named_scope("return_result"):
        parts = combine(part_keep, part_send)
        result = reduce_y(parts)
    with jax.named_scope("backward"):
        back_send = backward(down_sends, slope_send, BF)
        back_keep = backward(down_keeps, slope_keep, F32, parts[3])
    with jax.named_scope("return_back"):
        back = reduce_y(combine(back_keep, back_send))
    with jax.named_scope("collect"):
        ready = call(
            pack_kernel,
            sds((packed, WIDE), BF),
            [VMEM] * 6,
            [pltpu.VMEM((packed, WIDE), BF)],
            flops=10**8,
            moved=10**6,
        )(*result, *back)
        mine = exchange(ready)
        theirs = swap_core(mine)
    with jax.named_scope("final"):
        first = call(first_kernel, sds((4 * rows, WIDE), F32), [VMEM] * 3, flops=10**9, moved=4 * 10**6)(
            mine, merge_high, merge_low
        )
        layer_out, stream_grad = call(
            final_kernel,
            [sds((rows, width), BF)] * 2,
            [VMEM] * 7,
            [pltpu.VMEM((rows, width), F32)],
            flops=10**9,
            moved=4 * 10**6,
        )(first, theirs, merge_high, merge_low, stream, gain, upstream)
    return (layer_out, stream_grad)


def solution(mesh):
    sizes = mesh.devices.shape
    shards = 4
    split = Mesh(
        mesh.devices.reshape(sizes[0] // shards, shards, sizes[1]), ("xz", "y", "core")
    )
    return jax.shard_map(
        per_device,
        mesh=split,
        in_specs=(
            P(("xz", "y"), "core"),
            P("core", None),
            P(("xz", "y", "core"), None),
            P(),
            P(("xz", "y"), None, "core"),
            P(("xz", "y"), "core", None),
            P(),
            P(),
            P(),
            P(("xz", "y", "core"), None),
        ),
        out_specs=(P(("xz", "y", "core"), None), P(("xz", "y", "core"), None)),
        check_vma=False,
    )
```

```python
import functools

import jax
import jax.numpy as jnp
from jax import lax
from jax.experimental import pallas as pl
from jax.experimental.pallas import tpu as pltpu
from jax.sharding import Mesh, PartitionSpec as P

SLOTS = 4
HALF = 2
BF = jnp.bfloat16
F32 = jnp.float32
I32 = jnp.int32
VMEM = pl.BlockSpec(memory_space=pltpu.VMEM)
SMEM = pl.BlockSpec(memory_space=pltpu.SMEM)
ANY = pl.BlockSpec(memory_space=pl.ANY)
WIDE = 896
PACK = 8


def mm(a, b):
    return jnp.dot(a, b, preferred_element_type=F32)


def mm_t(a, b):
    return lax.dot_general(a, b, (((1,), (1,)), ((), ())), preferred_element_type=F32)


def mm_a(a, b):
    return lax.dot_general(a, b, (((0,), (0,)), ((), ())), preferred_element_type=F32)


def cuts(size, step):
    return [(i, min(i + step, size)) for i in range(0, size, step)]


def iota(shape, dim):
    return lax.broadcasted_iota(I32, shape, dim)


def call(kernel, outs, in_specs, scratch=(), flops=0, moved=0, mib=16):
    return pl.pallas_call(
        kernel,
        out_shape=outs,
        in_specs=in_specs,
        out_specs=jax.tree.map(lambda _: VMEM, outs),
        scratch_shapes=list(scratch),
        compiler_params=pltpu.CompilerParams(vmem_limit_bytes=mib * 2**20),
        cost_estimate=pl.CostEstimate(flops=flops, bytes_accessed=moved, transcendentals=0),
    )


def attend_kernel(other, ids, context, weight, out):
    at = (1 - ids[0]) if other else ids[0]
    rows = out.shape[0]
    block = context[:, pl.ds(pl.multiple_of(at * rows, rows), rows)]
    for lo, hi in cuts(out.shape[1], 512):
        out[:, lo:hi] = mm_a(block, weight[:, lo:hi])


def routing_kernel(ids, index, count, gate, pick_keep, pick_send, slots):
    core = ids[0]
    experts, capacity = index.shape
    packed = experts * PACK
    rows = pick_keep.shape[1] // 4
    local = index[...] - ids[1]
    diagonal = iota((experts, experts), 0) == iota((experts, experts), 1)
    counts = jnp.sum(jnp.where(diagonal, count[...].astype(F32), 0.0), axis=1, keepdims=True)
    listed = iota((experts, capacity), 1).astype(F32) < counts
    mine = listed & (local >= 0) & (local < 2 * rows)
    upto = jnp.where(iota((capacity, capacity), 0) <= iota((capacity, capacity), 1), 1.0, 0.0)
    rank = mm(jnp.where(mine, 1.0, 0.0).astype(BF), upto.astype(BF))
    lane = iota((experts, 128), 1)
    at_row = jnp.zeros((experts, 128), F32)
    gates = jnp.zeros((experts, 128), F32)
    shifted = (local + 1).astype(F32)
    for slot in range(SLOTS):
        here = mine & (rank == slot + 1.0)
        row = jnp.sum(jnp.where(here, shifted, 0.0), axis=1, keepdims=True) - 1.0
        at_row = jnp.where(lane == slot, row, at_row)
        value = jnp.sum(jnp.where(here, gate[...], 0.0), axis=1, keepdims=True)
        gates = jnp.where(lane == slot, value, gates)
    at_row = at_row.astype(BF)
    gate_high = gates.astype(BF)
    slots[:experts, :] = at_row
    slots[experts : 2 * experts, :] = gate_high
    slots[2 * experts :, :] = (gates - gate_high.astype(F32)).astype(BF)
    down = mm(spread_of(experts), at_row)
    r_col = iota((packed, 128), 0) % PACK
    lane_id = iota((packed, 128), 1)
    k = iota((packed, 2 * rows), 1)
    r_wide = iota((packed, 2 * rows), 0) % PACK
    same_stream = (r_wide // 2) % 2 == k // rows
    patch = (core * rows + k % rows).astype(F32)
    for out, side in ((pick_keep, core), (pick_send, 1 - core)):
        slot = 2 * side + r_col % 2
        row = jnp.sum(jnp.where(lane_id == slot, down, 0.0), axis=1, keepdims=True)
        hot = same_stream & (row == patch)
        out[:, : 2 * rows] = jnp.where(hot & (r_wide < 4), 1.0, 0.0).astype(BF)
        out[:, 2 * rows :] = jnp.where(hot & (r_wide >= 4), 1.0, 0.0).astype(BF)


def spread_of(experts):
    shape = (experts * PACK, experts)
    return jnp.where(iota(shape, 0) // PACK == iota(shape, 1), 1.0, 0.0).astype(BF)


def merge_kernel(ids, slots, merge_high, merge_low):
    core = ids[0]
    experts = slots.shape[0] // 3
    packed = experts * PACK
    rows = merge_high.shape[0] // 4
    spread = spread_of(experts)
    across = [
        lax.dot_general(
            slots[i * experts : (i + 1) * experts, :],
            spread,
            (((0,), (1,)), ((), ())),
            preferred_element_type=F32,
        )
        for i in range(3)
    ]
    q = iota((128, packed), 1) % PACK
    sub = iota((128, packed), 0)
    own = (core * rows + iota((rows, packed), 0)).astype(F32)
    q_rows = iota((rows, packed), 1) % PACK
    for which, side in ((0, core), (1, 1 - core)):
        slot = 2 * side + q % 2
        row, high, low = (
            jnp.sum(jnp.where(sub == slot, part, 0.0), axis=0, keepdims=True) for part in across
        )
        hot = row == own
        for group in range(4):
            here = hot & (q_rows // 2 == group)
            at = (slice(group * rows, (group + 1) * rows), slice(which * packed, (which + 1) * packed))
            merge_high[at] = jnp.where(here, high, 0.0).astype(BF)
            merge_low[at] = jnp.where(here, low, 0.0).astype(BF)


def statistics(stream):
    mean = jnp.mean(stream, axis=-1, keepdims=True)
    centered = stream - mean
    variance = jnp.mean(centered * centered, axis=-1, keepdims=True)
    return centered, lax.rsqrt(variance + 1e-06)


def select(pick, both, out):
    count = both.shape[0]
    rest = both.shape[1] - WIDE
    first, second = pick[:, :count], pick[:, count:]
    out[:, :rest] = (mm(first, both[:, :rest]) + mm(second, both[:, WIDE:])).astype(BF)
    out[:, rest:] = mm(first, both[:, rest:WIDE]).astype(BF)


def norm_kernel(att_keep, att_got, residual, gain, upstream, pick_send, stream, both, send):
    rows = residual.shape[0]
    total = residual[...].astype(F32) + (att_keep[...] + att_got[...])
    stream[...] = total
    centered, inverse = statistics(total)
    both[:rows, :] = (gain[...] * centered * inverse).astype(BF)
    both[rows:, :] = upstream[...]
    select(pick_send, both, send)


def place(packed):
    q = packed
    return (q % 64 // 2) * PACK + q // 64 * 2 + q % 2


def unpack_kernel(got, first, second):
    n = got.shape[0]
    order = jnp.where(place(iota((n, n), 0)) == iota((n, n), 1), 1.0, 0.0).astype(BF)
    flat = mm(order, got[...]).astype(BF)
    quarter = n // 4
    rest = first.shape[1] - WIDE
    for stream, out in enumerate((first, second)):
        out[:, :WIDE] = flat[stream * quarter : (stream + 1) * quarter, :]
        out[:, WIDE:] = flat[(2 + stream) * quarter : (3 + stream) * quarter, :rest]


def pack_kernel(own_r, one_r, two_r, own_b, one_b, two_b, out, flat):
    n = out.shape[0]
    quarter = n // 4
    rest = own_r.shape[1] - WIDE
    flat[2 * quarter :, rest:] = jnp.zeros((2 * quarter, WIDE - rest), BF)
    for stream, (own, one, two) in enumerate(((own_r, one_r, two_r), (own_b, one_b, two_b))):
        total = (own[...] + one[...].astype(F32) + two[...].astype(F32)).astype(BF)
        flat[stream * quarter : (stream + 1) * quarter, :] = total[:, :WIDE]
        flat[(2 + stream) * quarter : (3 + stream) * quarter, :rest] = total[:, WIDE:]
    order = jnp.where(iota((n, n), 0) == place(iota((n, n), 1)), 1.0, 0.0).astype(BF)
    out[...] = mm(order, flat[...]).astype(BF)


def forward_kernel(x0, x1, x2, x3, w1, w2, *rest):
    slope, part, x, hidden = rest[-4:]
    block = x0.shape[0]
    for i, ref in enumerate((x0, x1, x2, x3)):
        x[i * block : (i + 1) * block, :] = ref[...]
    for lo, hi in cuts(hidden.shape[1], 256):
        v = mm(x[...], w1[:, lo:hi])
        square = v * v
        t = jnp.tanh(0.7978845608 * v * (1.0 + 0.044715 * square))
        gate = 0.5 + 0.5 * t
        hidden[:, lo:hi] = (v * gate).astype(BF)
        slope[:, lo:hi] = gate + 0.5 * v * (1.0 - t * t) * (0.7978845608 * (1.0 + 0.134145 * square))
    for lo, hi in cuts(part.shape[1], 512):
        part[:, lo:hi] = mm(hidden[...], w2[:, lo:hi]).astype(part.dtype)


def backward_kernel(x0, x1, x2, x3, w1, w2, slope, *rest):
    part, x, grad = rest[-3:]
    block = x0.shape[0]
    for i, ref in enumerate((x0, x1, x2, x3)):
        x[i * block : (i + 1) * block, :] = ref[...]
    for lo, hi in cuts(grad.shape[1], 256):
        grad[:, lo:hi] = (mm_t(x[...], w2[lo:hi, :]) * slope[:, lo:hi]).astype(BF)
    for lo, hi in cuts(part.shape[1], 512):
        part[:, lo:hi] = mm_t(grad[...], w1[lo:hi, :]).astype(part.dtype)


def combine_kernel(keep, got, own, one, two, far):
    block = own.shape[0]
    for i, out in enumerate((own, one, two, far)):
        at = slice(i * block, (i + 1) * block)
        out[...] = (keep[at, :] + got[at, :].astype(F32)).astype(out.dtype)


def add_kernel(a, b, out):
    out[...] = (a[...].astype(F32) + b[...].astype(F32)).astype(BF)


def merged(rows, merge_high, merge_low, group, size, lo):
    at = (slice(group * size, (group + 1) * size), slice(lo, lo + rows.shape[0]))
    return mm(merge_high[at], rows[...]) + mm(merge_low[at], rows[...])


def first_kernel(mine, merge_high, merge_low, out):
    size = out.shape[0] // 4
    for group in range(4):
        at = slice(group * size, (group + 1) * size)
        out[at, :] = merged(mine, merge_high, merge_low, group, size, 0)


def final_kernel(first, theirs, merge_high, merge_low, stream, gain, upstream, layer_out, stream_grad, back):
    rows, width = stream.shape
    n = theirs.shape[0]
    rest = width - WIDE
    total = stream[...]
    centered, inverse = statistics(total)
    x_hat = centered * inverse
    for group in range(4):
        at = slice(group * rows, (group + 1) * rows)
        summed = first[at, :] + merged(theirs, merge_high, merge_low, group, rows, n)
        cols = slice(0, WIDE) if group < 2 else slice(WIDE, width)
        summed = summed if group < 2 else summed[:, :rest]
        if group % 2 == 0:
            layer_out[:, cols] = (total[:, cols] + summed).astype(BF)
        else:
            back[:, cols] = summed
    scaled = gain[...] * back[...]
    mean = jnp.mean(scaled, axis=-1, keepdims=True)
    along = jnp.mean(scaled * x_hat, axis=-1, keepdims=True)
    pulled = inverse * (scaled - mean - x_hat * along)
    stream_grad[...] = (upstream[...].astype(F32) + pulled).astype(BF)


def per_device(
    context,
    out_weight,
    residual,
    norm_gain,
    expert_in,
    expert_out,
    patch_index,
    patch_count,
    gate_value,
    upstream,
):
    rows, width = residual.shape
    experts, capacity = patch_index.shape
    shards = lax.axis_size("y")
    packed = experts * PACK
    block = experts * HALF
    units = expert_in.shape[2]
    sds = jax.ShapeDtypeStruct
    core = lax.axis_index("core")
    index = lax.axis_index("xz") * shards + lax.axis_index("y")
    ids = jnp.stack([core, index * (2 * rows)]).astype(I32)
    gain = norm_gain.reshape(1, width)

    def swap_core(x):
        return lax.ppermute(x, "core", [(0, 1), (1, 0)])

    def ring(x, way):
        pairs = []
        for y in range(shards):
            for c in range(2):
                step = way if c == 0 else -way
                pairs.append((y * 2 + c, (y + step) % shards * 2 + c))
        return lax.ppermute(x, ("y", "core"), pairs)

    def exchange(x):
        got = lax.all_to_all(
            x.reshape(experts, PACK, WIDE), "xz", split_axis=0, concat_axis=0, tiled=True
        )
        return got.reshape(packed, WIDE)

    def attend(other):
        return call(
            functools.partial(attend_kernel, other),
            sds((rows, width), F32),
            [SMEM, VMEM, VMEM],
            flops=2 * rows * width * context.shape[1],
            moved=4 * 10**6,
        )(ids, context.T, out_weight)

    with jax.named_scope("attend"):
        att_got = swap_core(attend(True))
        att_keep = attend(False)
    with jax.named_scope("routing"):
        pick_keep, pick_send, slots = call(
            routing_kernel,
            [sds((packed, 4 * rows), BF)] * 2 + [sds((3 * experts, 128), BF)],
            [SMEM] + [VMEM] * 3,
            flops=10**9,
            moved=10**6,
        )(ids, patch_index, patch_count.reshape(1, experts), gate_value)
    with jax.named_scope("merge"):
        merge_high, merge_low = call(
            merge_kernel,
            [sds((4 * rows, 2 * packed), BF)] * 2,
            [SMEM, VMEM],
            flops=10**8,
            moved=10**6,
        )(ids, slots)
    with jax.named_scope("norm"):
        stream, both, send = call(
            norm_kernel,
            [sds((rows, width), F32), sds((2 * rows, width), BF), sds((packed, WIDE), BF)],
            [VMEM] * 6,
            flops=10**9,
            moved=3 * 10**6,
        )(att_keep, att_got, residual, gain, upstream, pick_send)
        keep = call(select, sds((packed, WIDE), BF), [VMEM] * 2, flops=10**9, moved=10**6)(
            pick_keep, both
        )
    with jax.named_scope("dispatch"):
        got = exchange(keep + swap_core(send))
        normed_rows, down_rows = call(
            unpack_kernel, [sds((block, width), BF)] * 2, [VMEM], flops=10**8, moved=10**6
        )(got)

    def gather_y(own):
        one = ring(own, 1)
        two = ring(own, -1)
        far = ring(one, 1)
        keeps = [own, one, two, far]
        return keeps, [swap_core(x) for x in keeps]

    def combine(keep_part, send_part):
        return call(
            combine_kernel,
            [sds((block, width), F32)] * 2 + [sds((block, width), BF)] * 2,
            [VMEM] * 2,
            flops=10**6,
            moved=4 * 10**6,
        )(keep_part, swap_core(send_part))

    def reduce_y(parts):
        own, one, two, far = parts
        from_two = ring(two, 1)
        from_far = ring(far, -1)
        one = call(add_kernel, sds((block, width), BF), [VMEM] * 2, flops=10**5, moved=10**6)(one, from_far)
        return own, ring(one, -1), from_two

    weight_in = expert_in[0]
    weight_out = expert_out[0]
    tall = shards * block
    flops = 16 * tall * width * units

    def forward(xs, kind, *after):
        return call(
            forward_kernel,
            [sds((tall, units), F32), sds((tall, width), kind)],
            [VMEM] * 6 + [ANY] * len(after),
            [pltpu.VMEM((tall, width), BF), pltpu.VMEM((tall, units), BF)],
            flops=flops,
            moved=10**7,
            mib=24,
        )(*xs, weight_in, weight_out, *after)

    def backward(xs, slope, kind, *after):
        return call(
            backward_kernel,
            sds((tall, width), kind),
            [VMEM] * 7 + [ANY] * len(after),
            [pltpu.VMEM((tall, width), BF), pltpu.VMEM((tall, units), BF)],
            flops=flops,
            moved=10**7,
            mib=24,
        )(*xs, weight_in, weight_out, slope, *after)

    with jax.named_scope("gather_normed"):
        keeps, sends = gather_y(normed_rows)
    with jax.named_scope("gather_down"):
        down_keeps, down_sends = gather_y(down_rows)
    with jax.named_scope("forward"):
        slope_keep, part_keep = forward(keeps, F32)
        slope_send, part_send = forward(sends, BF, slope_keep)
    with jax.named_scope("return_result"):
        parts = combine(part_keep, part_send)
        result = reduce_y(parts)
    with jax.named_scope("backward"):
        back_send = backward(down_sends, slope_send, BF)
        back_keep = backward(down_keeps, slope_keep, F32, parts[3])
    with jax.named_scope("return_back"):
        back = reduce_y(combine(back_keep, back_send))
    with jax.named_scope("collect"):
        ready = call(
            pack_kernel,
            sds((packed, WIDE), BF),
            [VMEM] * 6,
            [pltpu.VMEM((packed, WIDE), BF)],
            flops=10**8,
            moved=10**6,
        )(*result, *back)
        mine = exchange(ready)
        theirs = swap_core(mine)
    with jax.named_scope("final"):
        first = call(first_kernel, sds((4 * rows, WIDE), F32), [VMEM] * 3, flops=10**9, moved=4 * 10**6)(
            mine, merge_high, merge_low
        )
        layer_out, stream_grad = call(
            final_kernel,
            [sds((rows, width), BF)] * 2,
            [VMEM] * 7,
            [pltpu.VMEM((rows, width), F32)],
            flops=10**9,
            moved=4 * 10**6,
        )(first, theirs, merge_high, merge_low, stream, gain, upstream)
    return (layer_out, stream_grad)


def solution(mesh):
    sizes = mesh.devices.shape
    shards = 4
    split = Mesh(
        mesh.devices.reshape(sizes[0] // shards, shards, sizes[1]), ("xz", "y", "core")
    )
    return jax.shard_map(
        per_device,
        mesh=split,
        in_specs=(
            P(("xz", "y"), "core"),
            P("core", None),
            P(("xz", "y", "core"), None),
            P(),
            P(("xz", "y"), None, "core"),
            P(("xz", "y"), "core", None),
            P(),
            P(),
            P(),
            P(("xz", "y", "core"), None),
        ),
        out_specs=(P(("xz", "y", "core"), None), P(("xz", "y", "core"), None)),
        check_vma=False,
    )
```
